32 devices in a mesh: depth: 4 (over z), illum: 8 (over y, x, core).
Axes of the slice: x: 2, y: 2, z: 4, core: 2. Of those that a mesh axis runs over, the one named last changes fastest.
Arguments:
- amplitude: float32 [4, 256, 256], P('depth', 'illum'), may hold values from 0.92 to 1
- phase: float32 [4, 256, 256], P('depth', 'illum'), may hold values from -3.140625 to 3.140625
- kernel_phase: float32 [256, 256], replicated, may hold values from -3.140625 to 3.140625
- entry_field: float32 [2, 4, 8, 256, 256], P(None, 'depth', 'illum'), may hold values from -6 to 6
- cotangent: float32 [2, 8, 256, 256], P(None, 'illum'), may hold values from -6 to 6
Outputs:
- slice_grad: float32 [2, 4, 256, 256], P(None, 'depth', 'illum')
The draws below stay inside these ranges and needn't reach their ends.
All inputs are finite; a program needn't handle non-finite values.
Results may differ from the reference program's by a relative error of at most 0.0003.
Values sent between devices are 32-bit elements; how exact they have to be, the bound alone decides.
A program may use at most 64 MiB of HBM per device.

```python
import math
import jax
import jax.numpy as jnp
from jax import lax

GRID = 256
SLICE_DEV = 1
BLOCKS = 4
SLICES = 4
ANGLES = 8


def spiked(entries, key, source, target, blocks, factor):
    owner, partner = [(jnp.arange(entries.shape[position]) // (entries.shape[position] // blocks)).reshape([-1 if axis == position else 1 for axis in range(entries.ndim)]) for position in (source, target)]
    chosen = jax.random.permutation(key, blocks)[partner]
    strong = (owner == chosen) | (owner == (partner + blocks // 2) % blocks)
    return jnp.where(strong, factor * entries, entries)


def steps_of(key, extent, pieces, low, top_value):
    level = 1.0
    for axis_at, shards_of in pieces:
        steps = jax.random.uniform(jax.random.fold_in(jax.random.fold_in(key, 6), axis_at), (shards_of,), jnp.float32, low / len(pieces), top_value / len(pieces))
        level = level * jnp.repeat(jnp.exp(steps), extent[axis_at] // shards_of).reshape((-1,) + (1,) * (len(extent) - 1 - axis_at))
    return level


def scatter_about(rng, dims, spread, most, shards=(), dtype=jnp.bfloat16):
    gain = steps_of(rng, dims, shards, -0.22, 0.18) if shards else 1.0
    values = jax.random.normal(rng, dims, jnp.float32) * spread * gain
    return jnp.minimum(jnp.maximum(values, -most), most).astype(dtype)


def heavy_noise(rng, dims, deviation, limit, shards, heavy, held_as=jnp.bfloat16):
    values = deviation * jax.random.normal(rng, dims, jnp.float32)
    if shards:
        values = values * steps_of(rng, dims, shards, -0.22, 0.18)
    return jnp.clip(spiked(values, jax.random.fold_in(rng, 3), *heavy), -limit, limit).astype(held_as)


def setup_inputs(seed: int = 0) -> dict:
    keys = jax.random.split(jax.random.key(seed), 6)
    return {
        "amplitude": jnp.clip(0.92 + 0.07999998 * jax.random.uniform(keys[0], (SLICES, GRID, GRID), jnp.float32) ** steps_of(keys[0], (SLICES, GRID, GRID), ((0, 4), (1, 8)), -0.2, 0.2), 0.92, 1.0),
        "phase": jnp.clip(jax.random.uniform(keys[1], (SLICES, GRID, GRID), jnp.float32, -3.140625, 3.140625), -3.140625, 3.140625),
        "kernel_phase": jnp.clip(jax.random.uniform(keys[2], (GRID, GRID), jnp.float32, -3.140625, 3.140625), -3.140625, 3.140625),
        "entry_field": scatter_about(keys[3], (2, BLOCKS, ANGLES, GRID, GRID), 1.0, 6.0, ((1, 4), (2, 8)), jnp.float32),
        "cotangent": heavy_noise(keys[4], (2, ANGLES, GRID, GRID), 1.0, 6.0, ((1, 8),), (1, 2, 8, 2.0), jnp.float32),
    }


def propagate(field, kernel):
    return jnp.fft.ifft2(kernel * jnp.fft.fft2(field))

def reference(amplitude, phase, kernel_phase, entry_field, cotangent):
    trans = lax.complex(amplitude * jnp.cos(phase), amplitude * jnp.sin(phase))
    kernel = lax.complex(jnp.cos(kernel_phase), jnp.sin(kernel_phase))
    chi = lax.complex(cotangent[0], cotangent[1])
    grads = [None] * (BLOCKS * SLICE_DEV)
    for block in reversed(range(BLOCKS)):
        field = lax.complex(entry_field[0, block], entry_field[1, block])
        seen = [field]
        for layer in range(SLICE_DEV - 1):
            field = propagate(trans[block * SLICE_DEV + layer] * field, kernel)
            seen.append(field)
        for layer in reversed(range(SLICE_DEV)):
            slot = block * SLICE_DEV + layer
            back = propagate(chi, jnp.conj(kernel))
            grads[slot] = lax.optimization_barrier(jnp.sum(back * jnp.conj(seen[layer]), axis=0)) / math.sqrt(ANGLES)
            chi = back * jnp.conj(trans[slot])
    total = jnp.stack(grads)
    return jnp.stack([jnp.real(total), jnp.imag(total)]).astype(jnp.float32)
```

```python
import functools
import math

import jax
import jax.numpy as jnp
import ml_dtypes
import numpy as np
from jax import lax
from jax.experimental import pallas as pl
from jax.experimental.pallas import tpu as pltpu
from jax.sharding import PartitionSpec as P

MESH = pl.DeviceIdType.MESH
F32 = jnp.float32
BF16 = jnp.bfloat16


def halves(matrix):
    high = matrix.astype(ml_dtypes.bfloat16)
    low = (matrix - high.astype(np.float64)).astype(ml_dtypes.bfloat16)
    return [high, low]


def tables(length):
    half = length // 2
    out = []
    for odd in (0, 1):
        k = 2 * np.arange(half)[:, None] + odd
        angle = (k * np.arange(half)[None, :] % length) * (2.0 * np.pi / length)
        c, s = np.cos(angle), np.sin(angle)
        out.append(np.block([[c, s], [-s, c]]))
    out += [out[0].T, out[1].T]
    perm = np.concatenate([np.arange(0, length, 2), np.arange(1, length, 2)])
    shuffle = np.zeros((length, length))
    shuffle[perm, np.arange(length)] = 1.0
    stacked = sum([halves(m) for m in out], [])
    return np.stack(stacked + [shuffle.astype(ml_dtypes.bfloat16)])


def sincos(x):
    y = x * 0.5
    z = y * y
    s = 1.0 / math.factorial(13)
    for order in (11, 9, 7, 5, 3, 1):
        s = s * z + (-1.0) ** (order // 2) / math.factorial(order)
    s = s * y
    c = 1.0 / math.factorial(12)
    for order in (10, 8, 6, 4, 2, 0):
        c = c * z + (-1.0) ** (order // 2) / math.factorial(order)
    return 2.0 * s * c, 1.0 - 2.0 * s * s


def split(v):
    high = v.astype(BF16)
    return high, (v - high.astype(F32)).astype(BF16)


def dot(a, b):
    return jnp.dot(a, b, preferred_element_type=F32)


def right(v, tab, at):
    high, low = split(v)
    w_high, w_low = tab[2 * at], tab[2 * at + 1]
    return dot(low, w_high) + dot(high, w_low) + dot(high, w_high)


def left(v, tab, at):
    high, low = split(v)
    w_high, w_low = tab[2 * at], tab[2 * at + 1]
    return dot(w_high, low) + dot(w_low, high) + dot(w_high, high)


def kernel(
    depth, count, amp_ref, phase_ref, kern_ref, psi_ref, cot_ref, tab, out_ref,
    x_ref, h_ref, tmp_ref, own_ref, t_ref, prod_ref, land_ref,
    z_send, z_recv, g_send, g_recv, r_send, r_recv,
):
    length = kern_ref.shape[0]
    half = length // 2
    rows = amp_ref.shape[0]
    bits = count.bit_length() - 1
    d = lax.axis_index("depth")
    me = lax.axis_index("illum")
    needed = depth - 1 - d

    flip = [(1 << b) * (1 - 2 * (me // (1 << b) % 2)) for b in range(bits)]
    core = me % 2
    ahead, other = [], []
    for r in range(bits - 1):
        down, up = flip[bits - 1 - r], flip[1 + r]
        ahead.append(down + core * (up - down))
        other.append(up + core * (down - up))
    if bits:
        ahead.append(flip[0])

    def owner(p):
        order = other if p >= count // 2 else ahead
        block = me
        for r in range(bits):
            if p >> r & 1:
                block = block + (ahead[r] if r == bits - 1 else order[r])
        return block

    def rows_of(p):
        return pl.ds(pl.multiple_of(owner(p) * rows, rows), rows)

    barrier = pltpu.get_barrier_semaphore()
    for o in range(1, depth):
        pl.semaphore_signal(barrier, inc=1, device_id=((d + o) % depth, me), device_id_type=MESH)
    for r in range(bits):
        pl.semaphore_signal(barrier, inc=1, device_id=(d, me + ahead[r]), device_id_type=MESH)

    sin_t, cos_t = sincos(phase_ref[...])
    own_ref[0] = amp_ref[...] * cos_t
    own_ref[1] = amp_ref[...] * sin_t

    pl.semaphore_wait(barrier, depth - 1 + bits)

    def z_copy(target):
        return pltpu.make_async_remote_copy(
            src_ref=own_ref, dst_ref=t_ref.at[needed, 0],
            send_sem=z_send.at[target], recv_sem=z_recv.at[needed],
            device_id=(target, me), device_id_type=MESH,
        )

    @pl.loop(0, d)
    def _(target):
        z_copy(target).start()

    def g_copy(s, r):
        w = 1 << r
        return pltpu.make_async_remote_copy(
            src_ref=t_ref.at[s, pl.ds(0, w)], dst_ref=t_ref.at[s, pl.ds(w, w)],
            send_sem=g_send.at[s, r], recv_sem=g_recv.at[s, r],
            device_id=(d, me + ahead[r]), device_id_type=MESH,
        )

    def advance(s, step):
        @pl.when(jnp.logical_and(s >= 0, s < needed))
        def _():
            if step == 0:
                pltpu.make_async_copy(own_ref, t_ref.at[s, 0], z_recv.at[s]).wait()
            else:
                g_copy(s, step - 1).wait_recv()
            if step < bits:
                g_copy(s, step).start()

    phase = kern_ref[...]
    first, rest = split(phase)
    rest = phase - first.astype(F32)
    second, third = split(rest)
    shuffle = tab[8]
    moved = (dot(third, shuffle) + dot(second, shuffle)) + dot(first, shuffle)
    tmp_ref[0], tmp_ref[1] = moved[:, :half], moved[:, half:]
    scale = 1.0 / (length * length)
    for odd in (0, 1):
        for c in (0, 1):
            sin_h, cos_h = sincos(tmp_ref[c, pl.ds(odd, half, stride=2), :])
            at = (pl.ds(odd * half, half), pl.ds(c * half, half))
            h_ref[(0, *at)] = cos_h * scale
            h_ref[(1, *at)] = sin_h * scale

    x_ref[0] = cot_ref[0]
    x_ref[1] = cot_ref[1]

    def propagate(slot):
        re, im = x_ref[0], x_ref[1]
        parts = []
        for sign, at in ((1, 2), (-1, 3)):
            mixed = jnp.concatenate(
                [v[:, :half] + sign * v[:, half:] for v in (re, im)], axis=1)
            parts.append(right(mixed, tab, at))
        slot(0)
        even, odd = parts
        back = []
        mixes = []
        for sign, at in ((1, 0), (-1, 1)):
            stack = jnp.concatenate([
                jnp.concatenate([
                    v[:half, c * half:(c + 1) * half] + sign * v[half:, c * half:(c + 1) * half]
                    for v in (even, odd)], axis=1)
                for c in (0, 1)], axis=0)
            freq = left(stack, tab, at)
            f_re, f_im = freq[:half], freq[half:]
            h_re = h_ref[0, at * half:(at + 1) * half]
            h_im = h_ref[1, at * half:(at + 1) * half]
            mixes.append(jnp.concatenate(
                [f_re * h_re + f_im * h_im, f_im * h_re - f_re * h_im], axis=0))
        slot(1)
        for at in (0, 1):
            back.append(left(mixes[at], tab, 2 + at))
        slot(2)
        e, o = back
        total, gap = e + o, e - o
        ends = []
        for c in (0, 1):
            cols = slice(c * half, (c + 1) * half)
            mixed = jnp.concatenate([
                jnp.concatenate([total[:half, cols], gap[:half, cols]], axis=0),
                jnp.concatenate([total[half:, cols], gap[half:, cols]], axis=0)], axis=1)
            ends.append(right(mixed, tab, c))
        e, o = ends
        total, gap = e + o, e - o
        x_ref[0, :, :half] = total[:, :half]
        x_ref[0, :, half:] = gap[:, :half]
        x_ref[1, :, :half] = total[:, half:]
        x_ref[1, :, half:] = gap[:, half:]
        slot(3)

    slots = max(4, bits + 1)

    def body(q, carry):
        def slot(k):
            for step in reversed(range(bits + 1)):
                advance(q * slots + k - step, step)

        propagate(slot)
        for k in range(4, slots):
            slot(k)
        for p in range(count):
            at = rows_of(p)
            t_re, t_im = t_ref[q, p, 0], t_ref[q, p, 1]
            u_re, u_im = x_ref[0, at], x_ref[1, at]
            x_ref[0, at] = u_re * t_re + u_im * t_im
            x_ref[1, at] = u_im * t_re - u_re * t_im
        return carry

    lax.fori_loop(0, needed, body, 0)
    propagate(lambda k: None)

    def product(p):
        at = rows_of(p)
        u_re, u_im = x_ref[0, at], x_ref[1, at]
        p_re, p_im = psi_ref[0, at], psi_ref[1, at]
        prod_ref[p, 0] = u_re * p_re + u_im * p_im
        prod_ref[p, 1] = u_im * p_re - u_re * p_im

    def r_copy(r):
        w = 1 << r
        return pltpu.make_async_remote_copy(
            src_ref=prod_ref.at[pl.ds(w, w)], dst_ref=land_ref.at[pl.ds(w, w)],
            send_sem=r_send.at[r], recv_sem=r_recv.at[r],
            device_id=(d, me + ahead[r]), device_id_type=MESH,
        )

    for p in range(count // 2, count):
        product(p)
    if bits:
        r_copy(bits - 1).start()
    for p in range(count // 2):
        product(p)
    for r in reversed(range(bits)):
        w = 1 << r
        r_copy(r).wait_recv()
        if r:
            v = w // 2
            prod_ref[v:w] += land_ref[w + v:2 * w]
            r_copy(r - 1).start()
            prod_ref[:v] += land_ref[w:w + v]
        else:
            prod_ref[0] += land_ref[1]
    out_ref[...] = prod_ref[0]

    for r in range(bits):
        r_copy(r).wait_send()

    @pl.loop(0, needed)
    def _(s):
        for r in range(bits):
            g_copy(s, r).wait_send()

    @pl.loop(0, d)
    def _(target):
        z_copy(target).wait_send()


def per_device(depth, count, amplitude, phase, kernel_phase, entry_field, cotangent):
    _, rows, length = amplitude.shape
    angles = entry_field.shape[2]
    assert angles == 1 and amplitude.shape[0] == 1
    bits = count.bit_length() - 1
    assert count == 1 << bits
    above, steps = max(depth - 1, 1), max(bits, 1)
    tab = jnp.asarray(tables(length))
    vmem = pl.BlockSpec(memory_space=pltpu.VMEM)
    field = (2, length, length)
    dma = pltpu.SemaphoreType.DMA
    mine = pl.pallas_call(
        functools.partial(kernel, depth, count),
        out_shape=jax.ShapeDtypeStruct((2, rows, length), F32),
        in_specs=[vmem] * 6,
        out_specs=vmem,
        scratch_shapes=[
            pltpu.VMEM(field, F32),
            pltpu.VMEM(field, F32),
            pltpu.VMEM((2, length, length // 2), F32),
            pltpu.VMEM((2, rows, length), F32),
            pltpu.VMEM((above, count, 2, rows, length), F32),
            pltpu.VMEM((count, 2, rows, length), F32),
            pltpu.VMEM((count, 2, rows, length), F32),
            dma((above,)), dma((above,)),
            dma((above, steps)), dma((above, steps)),
            dma((steps,)), dma((steps,)),
        ],
        compiler_params=pltpu.CompilerParams(
            collective_id=0, has_side_effects=True, vmem_limit_bytes=40 * 1024 * 1024),
    )(amplitude[0], phase[0], kernel_phase, entry_field[:, 0, 0], cotangent[:, 0], tab)
    return (mine * (1.0 / math.sqrt(angles * count)))[:, None]


def solution(mesh):
    return jax.shard_map(
        functools.partial(per_device, mesh.shape["depth"], mesh.shape["illum"]),
        mesh=mesh,
        in_specs=(
            P("depth", "illum", None),
            P("depth", "illum", None),
            P(),
            P(None, "depth", "illum", None, None),
            P(None, "illum", None, None),
        ),
        out_specs=P(None, "depth", "illum", None),
        check_vma=False,
    )
```

```python
import functools
import math

import jax
import jax.numpy as jnp
import ml_dtypes
import numpy as np
from jax import lax
from jax.experimental import pallas as pl
from jax.experimental.pallas import tpu as pltpu
from jax.sharding import PartitionSpec as P

MESH = pl.DeviceIdType.MESH
F32 = jnp.float32
BF16 = jnp.bfloat16


def halves(matrix):
    high = matrix.astype(ml_dtypes.bfloat16)
    low = (matrix - high.astype(np.float64)).astype(ml_dtypes.bfloat16)
    return [high, low]


def tables(length):
    half = length // 2
    out = []
    for odd in (0, 1):
        k = 2 * np.arange(half)[:, None] + odd
        angle = (k * np.arange(half)[None, :] % length) * (2.0 * np.pi / length)
        c, s = np.cos(angle), np.sin(angle)
        out.append(np.block([[c, s], [-s, c]]))
    out += [out[0].T, out[1].T]
    perm = np.concatenate([np.arange(0, length, 2), np.arange(1, length, 2)])
    shuffle = np.zeros((length, length))
    shuffle[perm, np.arange(length)] = 1.0
    stacked = sum([halves(m) for m in out], [])
    return np.stack(stacked + [shuffle.astype(ml_dtypes.bfloat16)])


def sincos(x):
    y = x * 0.5
    z = y * y
    s = 1.0 / math.factorial(13)
    for order in (11, 9, 7, 5, 3, 1):
        s = s * z + (-1.0) ** (order // 2) / math.factorial(order)
    s = s * y
    c = 1.0 / math.factorial(12)
    for order in (10, 8, 6, 4, 2, 0):
        c = c * z + (-1.0) ** (order // 2) / math.factorial(order)
    return 2.0 * s * c, 1.0 - 2.0 * s * s


def split(v):
    high = v.astype(BF16)
    return high, (v - high.astype(F32)).astype(BF16)


def dot(a, b):
    return jnp.dot(a, b, preferred_element_type=F32)


def right(v, tab, at):
    high, low = split(v)
    w_high, w_low = tab[2 * at], tab[2 * at + 1]
    return dot(low, w_high) + dot(high, w_low) + dot(high, w_high)


def left(v, tab, at):
    high, low = split(v)
    w_high, w_low = tab[2 * at], tab[2 * at + 1]
    return dot(w_high, low) + dot(w_low, high) + dot(w_high, high)


def kernel(
    depth, count, amp_hbm, phase_hbm, kern_hbm, psi_hbm, cot_hbm, tab_hbm, out_ref,
    amp_ref, phase_ref, kern_ref, psi_ref, tab,
    x_ref, h_ref, tmp_ref, own_ref, t_ref, prod_ref, land_ref, loaded,
    z_send, z_recv, g_send, g_recv, r_send, r_recv,
):
    length = kern_ref.shape[0]
    half = length // 2
    rows = amp_ref.shape[0]
    bits = count.bit_length() - 1
    d = lax.axis_index("depth")
    me = lax.axis_index("illum")
    needed = depth - 1 - d

    loads = [
        pltpu.make_async_copy(source, target, loaded.at[i])
        for i, (source, target) in enumerate([
            (amp_hbm, amp_ref), (phase_hbm, phase_ref), (kern_hbm, kern_ref),
            (tab_hbm, tab), (cot_hbm, x_ref), (psi_hbm, psi_ref)])
    ]
    for load in loads:
        load.start()

    flip = [(1 << b) * (1 - 2 * (me // (1 << b) % 2)) for b in range(bits)]
    core = me % 2
    ahead, other = [], []
    for r in range(bits - 1):
        down, up = flip[bits - 1 - r], flip[1 + r]
        ahead.append(down + core * (up - down))
        other.append(up + core * (down - up))
    if bits:
        ahead.append(flip[0])

    def owner(p):
        order = other if p >= count // 2 else ahead
        block = me
        for r in range(bits):
            if p >> r & 1:
                block = block + (ahead[r] if r == bits - 1 else order[r])
        return block

    def rows_of(p):
        return pl.ds(pl.multiple_of(owner(p) * rows, rows), rows)

    barrier = pltpu.get_barrier_semaphore()
    for o in range(1, depth):
        pl.semaphore_signal(barrier, inc=1, device_id=((d + o) % depth, me), device_id_type=MESH)
    for r in range(bits):
        pl.semaphore_signal(barrier, inc=1, device_id=(d, me + ahead[r]), device_id_type=MESH)

    loads[0].wait()
    loads[1].wait()
    sin_t, cos_t = sincos(phase_ref[...])
    own_ref[0] = amp_ref[...] * cos_t
    own_ref[1] = amp_ref[...] * sin_t

    pl.semaphore_wait(barrier, depth - 1 + bits)

    def z_copy(target):
        return pltpu.make_async_remote_copy(
            src_ref=own_ref, dst_ref=t_ref.at[needed, 0],
            send_sem=z_send.at[target], recv_sem=z_recv.at[needed],
            device_id=(target, me), device_id_type=MESH,
        )

    def post(g):
        target = g + 1 - needed

        @pl.when(jnp.logical_and(target >= 0, target < d))
        def _():
            z_copy(target).start()

    post(-1)

    def g_copy(s, r):
        w = 1 << r
        return pltpu.make_async_remote_copy(
            src_ref=t_ref.at[s, pl.ds(0, w)], dst_ref=t_ref.at[s, pl.ds(w, w)],
            send_sem=g_send.at[s, r], recv_sem=g_recv.at[s, r],
            device_id=(d, me + ahead[r]), device_id_type=MESH,
        )

    def advance(s, step):
        @pl.when(jnp.logical_and(s >= 0, s < needed))
        def _():
            if step == 0:
                pltpu.make_async_copy(own_ref, t_ref.at[s, 0], z_recv.at[s]).wait()
            else:
                g_copy(s, step - 1).wait_recv()
            if step < bits:
                g_copy(s, step).start()

    loads[2].wait()
    loads[3].wait()
    phase = kern_ref[...]
    first, rest = split(phase)
    rest = phase - first.astype(F32)
    second, third = split(rest)
    shuffle = tab[8]
    moved = (dot(third, shuffle) + dot(second, shuffle)) + dot(first, shuffle)
    tmp_ref[0], tmp_ref[1] = moved[:, :half], moved[:, half:]
    scale = 1.0 / (length * length)
    for odd in (0, 1):
        for c in (0, 1):
            sin_h, cos_h = sincos(tmp_ref[c, pl.ds(odd, half, stride=2), :])
            at = (pl.ds(odd * half, half), pl.ds(c * half, half))
            h_ref[(0, *at)] = cos_h * scale
            h_ref[(1, *at)] = sin_h * scale

    loads[4].wait()

    def propagate(slot):
        re, im = x_ref[0], x_ref[1]
        parts = []
        for sign, at in ((1, 2), (-1, 3)):
            mixed = jnp.concatenate(
                [v[:, :half] + sign * v[:, half:] for v in (re, im)], axis=1)
            parts.append(right(mixed, tab, at))
        slot(0)
        even, odd = parts
        back = []
        mixes = []
        for sign, at in ((1, 0), (-1, 1)):
            stack = jnp.concatenate([
                jnp.concatenate([
                    v[:half, c * half:(c + 1) * half] + sign * v[half:, c * half:(c + 1) * half]
                    for v in (even, odd)], axis=1)
                for c in (0, 1)], axis=0)
            freq = left(stack, tab, at)
            f_re, f_im = freq[:half], freq[half:]
            h_re = h_ref[0, at * half:(at + 1) * half]
            h_im = h_ref[1, at * half:(at + 1) * half]
            mixes.append(jnp.concatenate(
                [f_re * h_re + f_im * h_im, f_im * h_re - f_re * h_im], axis=0))
        slot(1)
        for at in (0, 1):
            back.append(left(mixes[at], tab, 2 + at))
        slot(2)
        e, o = back
        total, gap = e + o, e - o
        ends = []
        for c in (0, 1):
            cols = slice(c * half, (c + 1) * half)
            mixed = jnp.concatenate([
                jnp.concatenate([total[:half, cols], gap[:half, cols]], axis=0),
                jnp.concatenate([total[half:, cols], gap[half:, cols]], axis=0)], axis=1)
            ends.append(right(mixed, tab, c))
        e, o = ends
        total, gap = e + o, e - o
        x_ref[0, :, :half] = total[:, :half]
        x_ref[0, :, half:] = gap[:, :half]
        x_ref[1, :, :half] = total[:, half:]
        x_ref[1, :, half:] = gap[:, half:]
        slot(3)

    slots = max(4, bits + 1 + (bits + 1) % 2)

    def slot(q, k):
        post(q * slots + k)
        for step in reversed(range(bits + 1)):
            if (k - step) % 2 == 0:
                advance(q * (slots // 2) + (k - step) // 2, step)

    def body(q, carry):
        propagate(functools.partial(slot, q))
        for k in range(4, slots):
            slot(q, k)
        for p in range(count):
            at = rows_of(p)
            t_re, t_im = t_ref[q, p, 0], t_ref[q, p, 1]
            u_re, u_im = x_ref[0, at], x_ref[1, at]
            x_ref[0, at] = u_re * t_re + u_im * t_im
            x_ref[1, at] = u_im * t_re - u_re * t_im
        return carry

    lax.fori_loop(0, needed, body, 0)
    propagate(lambda k: post(needed * slots + k))

    @pl.loop(jnp.minimum(needed * slots + 5 - needed, d), d)
    def _(target):
        z_copy(target).start()

    loads[5].wait()

    def product(p):
        at = rows_of(p)
        u_re, u_im = x_ref[0, at], x_ref[1, at]
        p_re, p_im = psi_ref[0, at], psi_ref[1, at]
        prod_ref[p, 0] = u_re * p_re + u_im * p_im
        prod_ref[p, 1] = u_im * p_re - u_re * p_im

    def r_copy(r):
        w = 1 << r
        return pltpu.make_async_remote_copy(
            src_ref=prod_ref.at[pl.ds(w, w)], dst_ref=land_ref.at[pl.ds(w, w)],
            send_sem=r_send.at[r], recv_sem=r_recv.at[r],
            device_id=(d, me + ahead[r]), device_id_type=MESH,
        )

    for p in range(count // 2, count):
        product(p)
    if bits:
        r_copy(bits - 1).start()
    for p in range(count // 2):
        product(p)
    for r in reversed(range(bits)):
        w = 1 << r
        r_copy(r).wait_recv()
        if r:
            v = w // 2
            prod_ref[v:w] += land_ref[w + v:2 * w]
            r_copy(r - 1).start()
            prod_ref[:v] += land_ref[w:w + v]
        else:
            prod_ref[0] += land_ref[1]
    out_ref[...] = prod_ref[0]

    for r in range(bits):
        r_copy(r).wait_send()

    @pl.loop(0, needed)
    def _(s):
        for r in range(bits):
            g_copy(s, r).wait_send()

    @pl.loop(0, d)
    def _(target):
        z_copy(target).wait_send()


def per_device(depth, count, amplitude, phase, kernel_phase, entry_field, cotangent):
    _, rows, length = amplitude.shape
    angles = entry_field.shape[2]
    assert angles == 1 and amplitude.shape[0] == 1
    bits = count.bit_length() - 1
    assert count == 1 << bits
    above, steps = max(depth - 1, 1), max(bits, 1)
    tab = jnp.asarray(tables(length))
    field = (2, length, length)
    dma = pltpu.SemaphoreType.DMA
    mine = pl.pallas_call(
        functools.partial(kernel, depth, count),
        out_shape=jax.ShapeDtypeStruct((2, rows, length), F32),
        in_specs=[pl.BlockSpec(memory_space=pl.ANY)] * 6,
        out_specs=pl.BlockSpec(memory_space=pltpu.VMEM),
        scratch_shapes=[
            pltpu.VMEM((rows, length), F32),
            pltpu.VMEM((rows, length), F32),
            pltpu.VMEM((length, length), F32),
            pltpu.VMEM(field, F32),
            pltpu.VMEM(tab.shape, BF16),
            pltpu.VMEM(field, F32),
            pltpu.VMEM(field, F32),
            pltpu.VMEM((2, length, length // 2), F32),
            pltpu.VMEM((2, rows, length), F32),
            pltpu.VMEM((above, count, 2, rows, length), F32),
            pltpu.VMEM((count, 2, rows, length), F32),
            pltpu.VMEM((count, 2, rows, length), F32),
            dma((6,)),
            dma((above,)), dma((above,)),
            dma((above, steps)), dma((above, steps)),
            dma((steps,)), dma((steps,)),
        ],
        compiler_params=pltpu.CompilerParams(
            collective_id=0, has_side_effects=True, vmem_limit_bytes=60 * 1024 * 1024),
    )(amplitude[0], phase[0], kernel_phase, entry_field[:, 0, 0], cotangent[:, 0], tab)
    return (mine * (1.0 / math.sqrt(angles * count)))[:, None]


def solution(mesh):
    return jax.shard_map(
        functools.partial(per_device, mesh.shape["depth"], mesh.shape["illum"]),
        mesh=mesh,
        in_specs=(
            P("depth", "illum", None),
            P("depth", "illum", None),
            P(),
            P(None, "depth", "illum", None, None),
            P(None, "illum", None, None),
        ),
        out_specs=P(None, "depth", "illum", None),
        check_vma=False,
    )
```

```python
import functools
import math

import jax
import jax.numpy as jnp
import ml_dtypes
import numpy as np
from jax import lax
from jax.experimental import pallas as pl
from jax.experimental.pallas import tpu as pltpu
from jax.sharding import PartitionSpec as P

MESH = pl.DeviceIdType.MESH
F32 = jnp.float32
BF16 = jnp.bfloat16


def halves(matrix):
    high = matrix.astype(ml_dtypes.bfloat16)
    low = (matrix - high.astype(np.float64)).astype(ml_dtypes.bfloat16)
    return [high, low]


def tables(length):
    half = length // 2
    out = []
    for odd in (0, 1):
        k = 2 * np.arange(half)[:, None] + odd
        angle = (k * np.arange(half)[None, :] % length) * (2.0 * np.pi / length)
        c, s = np.cos(angle), np.sin(angle)
        out.append(np.block([[c, s], [-s, c]]))
    out += [out[0].T, out[1].T]
    perm = np.concatenate([np.arange(0, length, 2), np.arange(1, length, 2)])
    shuffle = np.zeros((length, length))
    shuffle[perm, np.arange(length)] = 1.0
    stacked = sum([halves(m) for m in out], [])
    return np.stack(stacked + [shuffle.astype(ml_dtypes.bfloat16)])


def sincos(x):
    y = x * 0.5
    z = y * y
    s = 1.0 / math.factorial(13)
    for order in (11, 9, 7, 5, 3, 1):
        s = s * z + (-1.0) ** (order // 2) / math.factorial(order)
    s = s * y
    c = 1.0 / math.factorial(12)
    for order in (10, 8, 6, 4, 2, 0):
        c = c * z + (-1.0) ** (order // 2) / math.factorial(order)
    return 2.0 * s * c, 1.0 - 2.0 * s * s


def split(v):
    high = v.astype(BF16)
    return high, (v - high.astype(F32)).astype(BF16)


def dot(a, b):
    return jnp.dot(a, b, preferred_element_type=F32)


def right(v, tab, at):
    high, low = split(v)
    w_high, w_low = tab[2 * at], tab[2 * at + 1]
    return dot(low, w_high) + dot(high, w_low) + dot(high, w_high)


def left(v, tab, at):
    high, low = split(v)
    w_high, w_low = tab[2 * at], tab[2 * at + 1]
    return dot(w_high, low) + dot(w_low, high) + dot(w_high, high)


def kernel(
    depth, count, amp_hbm, phase_hbm, kern_hbm, psi_hbm, cot_hbm, tab_hbm, out_ref,
    amp_ref, phase_ref, kern_ref, psi_ref, tab,
    x_ref, h_ref, tmp_ref, own_ref, t_ref, end_ref, give_ref, got_ref, keep_ref, land_ref, loaded,
    z_send, z_recv, g_send, g_recv, c_send, c_recv, twin_send, twin_recv, r_send, r_recv,
):
    length = kern_ref.shape[0]
    half = length // 2
    rows = amp_ref.shape[0]
    chips = count // 2
    d = lax.axis_index("depth")
    me = lax.axis_index("illum")
    chip, core = me // 2, me % 2
    needed = depth - 1 - d

    loads = [
        pltpu.make_async_copy(source, target, loaded.at[i])
        for i, (source, target) in enumerate([
            (amp_hbm, amp_ref), (phase_hbm, phase_ref), (kern_hbm, kern_ref),
            (tab_hbm, tab), (cot_hbm, x_ref), (psi_hbm, psi_ref)])
    ]
    for load in loads:
        load.start()

    def near(p):
        return (chip + p) % chips

    def owner(p):
        if p < chips:
            return 2 * near(p) + core
        return 2 * near(p - chips) + 1 - core

    def rows_of(p):
        return pl.ds(pl.multiple_of(owner(p) * rows, rows), rows)

    twin = (d, 2 * chip + 1 - core)
    barrier = pltpu.get_barrier_semaphore()
    for o in range(1, depth):
        pl.semaphore_signal(barrier, inc=1, device_id=((d + o) % depth, me), device_id_type=MESH)
    for p in range(1, chips + 1):
        peer = (d, owner(p)) if p < chips else twin
        pl.semaphore_signal(barrier, inc=1, device_id=peer, device_id_type=MESH)

    loads[0].wait()
    loads[1].wait()
    sin_t, cos_t = sincos(phase_ref[...])
    own_ref[0] = amp_ref[...] * cos_t
    own_ref[1] = amp_ref[...] * sin_t

    pl.semaphore_wait(barrier, depth - 1 + chips)

    def z_copy(target):
        return pltpu.make_async_remote_copy(
            src_ref=own_ref, dst_ref=t_ref.at[needed, 0],
            send_sem=z_send.at[target], recv_sem=z_recv.at[needed],
            device_id=(target, me), device_id_type=MESH,
        )

    def post(g):
        target = g + 1 - needed

        @pl.when(jnp.logical_and(target >= 0, target < d))
        def _():
            z_copy(target).start()

    post(-1)

    def g_copy(s, p):
        return pltpu.make_async_remote_copy(
            src_ref=t_ref.at[s, 0], dst_ref=t_ref.at[s, chips - p],
            send_sem=g_send.at[s, p], recv_sem=g_recv.at[s, chips - p],
            device_id=(d, owner(p)), device_id_type=MESH,
        )

    def c_copy(s, first, size):
        which = min(first, 1)
        return pltpu.make_async_remote_copy(
            src_ref=t_ref.at[s, pl.ds(first, size)],
            dst_ref=t_ref.at[s, pl.ds(chips + first, size)],
            send_sem=c_send.at[s, which], recv_sem=c_recv.at[s, which],
            device_id=twin, device_id_type=MESH,
        )

    def advance(s, step):
        @pl.when(s < needed)
        def _():
            if step == 0:
                pltpu.make_async_copy(own_ref, t_ref.at[s, 0], z_recv.at[s]).wait()
                for p in range(1, chips):
                    g_copy(s, p).start()
                c_copy(s, 0, 1).start()
            elif step == 1:
                for p in range(1, chips):
                    pltpu.make_async_copy(own_ref, t_ref.at[s, p], g_recv.at[s, p]).wait()
                if chips > 1:
                    c_copy(s, 1, chips - 1).start()
            else:
                c_copy(s, 0, 1).wait_recv()
                if chips > 1:
                    c_copy(s, 1, chips - 1).wait_recv()

    loads[2].wait()
    loads[3].wait()
    phase = kern_ref[...]
    first, rest = split(phase)
    rest = phase - first.astype(F32)
    second, third = split(rest)
    shuffle = tab[8]
    moved = (dot(third, shuffle) + dot(second, shuffle)) + dot(first, shuffle)
    tmp_ref[0], tmp_ref[1] = moved[:, :half], moved[:, half:]
    scale = 1.0 / (length * length)
    for odd in (0, 1):
        for c in (0, 1):
            sin_h, cos_h = sincos(tmp_ref[c, pl.ds(odd, half, stride=2), :])
            at = (pl.ds(odd * half, half), pl.ds(c * half, half))
            h_ref[(0, *at)] = cos_h * scale
            h_ref[(1, *at)] = sin_h * scale

    loads[4].wait()

    def propagate(slot):
        re, im = x_ref[0], x_ref[1]
        parts = []
        for sign, at in ((1, 2), (-1, 3)):
            mixed = jnp.concatenate(
                [v[:, :half] + sign * v[:, half:] for v in (re, im)], axis=1)
            parts.append(right(mixed, tab, at))
        slot(0)
        even, odd = parts
        back = []
        mixes = []
        for sign, at in ((1, 0), (-1, 1)):
            stack = jnp.concatenate([
                jnp.concatenate([
                    v[:half, c * half:(c + 1) * half] + sign * v[half:, c * half:(c + 1) * half]
                    for v in (even, odd)], axis=1)
                for c in (0, 1)], axis=0)
            freq = left(stack, tab, at)
            f_re, f_im = freq[:half], freq[half:]
            h_re = h_ref[0, at * half:(at + 1) * half]
            h_im = h_ref[1, at * half:(at + 1) * half]
            mixes.append(jnp.concatenate(
                [f_re * h_re + f_im * h_im, f_im * h_re - f_re * h_im], axis=0))
        slot(1)
        for at in (0, 1):
            back.append(left(mixes[at], tab, 2 + at))
        slot(2)
        e, o = back
        total, gap = e + o, e - o
        ends = []
        for c in (0, 1):
            cols = slice(c * half, (c + 1) * half)
            mixed = jnp.concatenate([
                jnp.concatenate([total[:half, cols], gap[:half, cols]], axis=0),
                jnp.concatenate([total[half:, cols], gap[half:, cols]], axis=0)], axis=1)
            ends.append(mixed)
        return ends

    def finish(ends):
        e, o = [right(v, tab, at) for at, v in enumerate(ends)]
        total, gap = e + o, e - o
        return (
            jnp.concatenate([total[:, :half], gap[:, :half]], axis=1),
            jnp.concatenate([total[:, half:], gap[:, half:]], axis=1),
        )

    def slot(q, k):
        post(q * 4 + k)
        if k == 0:
            @pl.when(q == 0)
            def _():
                advance(q, 0)
        elif k == 1:
            advance(q, 1)
            advance(q + 1, 0)
        elif k == 3:
            advance(q, 2)

    def body(q, carry):
        x_ref[0], x_ref[1] = finish(propagate(functools.partial(slot, q)))
        slot(q, 3)
        for p in range(count):
            at = rows_of(p)
            t_re, t_im = t_ref[q, p, 0], t_ref[q, p, 1]
            u_re, u_im = x_ref[0, at], x_ref[1, at]
            x_ref[0, at] = u_re * t_re + u_im * t_im
            x_ref[1, at] = u_im * t_re - u_re * t_im
        return carry

    lax.fori_loop(0, needed, body, 0)
    ends = propagate(lambda k: post(needed * 4 + k))
    for c in (0, 1):
        end_ref[c] = ends[c].reshape(chips, 2, rows, length)

    @pl.loop(jnp.minimum(needed * 4 + 4 - needed, d), d)
    def _(target):
        z_copy(target).start()

    def products(to_ref, kind):
        flat = (chips * rows, length)
        u_re, u_im = finish([end_ref[c, :, kind].reshape(flat) for c in (0, 1)])
        p_re, p_im = [psi_ref[c, :, kind].reshape(flat) for c in (0, 1)]
        shape = (chips, rows, length)
        to_ref[:, 0] = (u_re * p_re + u_im * p_im).reshape(shape)
        to_ref[:, 1] = (u_im * p_re - u_re * p_im).reshape(shape)

    def twin_copy(p):
        at = near(p)
        return pltpu.make_async_remote_copy(
            src_ref=give_ref.at[at], dst_ref=got_ref.at[at],
            send_sem=twin_send.at[p], recv_sem=twin_recv.at[p],
            device_id=twin, device_id_type=MESH,
        )

    def sum_copy(p):
        return pltpu.make_async_remote_copy(
            src_ref=keep_ref.at[near(p)], dst_ref=land_ref.at[chips - p],
            send_sem=r_send.at[p], recv_sem=r_recv.at[chips - p],
            device_id=(d, owner(p)), device_id_type=MESH,
        )

    loads[5].wait()
    products(give_ref, 1 - core)
    order = [*range(1, chips), 0]
    for p in order:
        twin_copy(p).start()
    products(keep_ref, core)
    for p in order:
        twin_copy(p).wait_recv()
        if p:
            keep_ref[near(p)] += got_ref[near(p)]
            sum_copy(p).start()
    total = keep_ref[chip] + got_ref[chip]
    for p in range(1, chips):
        pltpu.make_async_copy(own_ref, land_ref.at[p], r_recv.at[p]).wait()
        total = total + land_ref[p]
    out_ref[...] = total

    for p in range(chips):
        twin_copy(p).wait_send()
        if p:
            sum_copy(p).wait_send()

    @pl.loop(0, needed)
    def _(s):
        for p in range(1, chips):
            g_copy(s, p).wait_send()
        c_copy(s, 0, 1).wait_send()
        if chips > 1:
            c_copy(s, 1, chips - 1).wait_send()

    @pl.loop(0, d)
    def _(target):
        z_copy(target).wait_send()


def per_device(depth, count, amplitude, phase, kernel_phase, entry_field, cotangent):
    _, rows, length = amplitude.shape
    angles = entry_field.shape[2]
    assert angles == 1 and amplitude.shape[0] == 1 and count % 2 == 0
    chips, above = count // 2, max(depth - 1, 1)
    tab = jnp.asarray(tables(length))
    field = (2, length, length)
    blocks = (2, chips, 2, rows, length)
    half_sum = (chips, 2, rows, length)
    dma = pltpu.SemaphoreType.DMA
    mine = pl.pallas_call(
        functools.partial(kernel, depth, count),
        out_shape=jax.ShapeDtypeStruct((2, rows, length), F32),
        in_specs=[pl.BlockSpec(memory_space=pltpu.HBM)] * 6,
        out_specs=pl.BlockSpec(memory_space=pltpu.VMEM),
        scratch_shapes=[
            pltpu.VMEM((rows, length), F32),
            pltpu.VMEM((rows, length), F32),
            pltpu.VMEM((length, length), F32),
            pltpu.VMEM(blocks, F32),
            pltpu.VMEM(tab.shape, BF16),
            pltpu.VMEM(field, F32),
            pltpu.VMEM(field, F32),
            pltpu.VMEM((2, length, length // 2), F32),
            pltpu.VMEM((2, rows, length), F32),
            pltpu.VMEM((above, count, 2, rows, length), F32),
            pltpu.VMEM(blocks, F32),
            pltpu.VMEM(half_sum, F32),
            pltpu.VMEM(half_sum, F32),
            pltpu.VMEM(half_sum, F32),
            pltpu.VMEM(half_sum, F32),
            dma((6,)),
            dma((above,)), dma((above,)),
            dma((above, chips)), dma((above, chips)),
            dma((above, 2)), dma((above, 2)),
            dma((chips,)), dma((chips,)), dma((chips,)), dma((chips,)),
        ],
        compiler_params=pltpu.CompilerParams(
            collective_id=0, has_side_effects=True, vmem_limit_bytes=24 * 1024 * 1024),
    )(amplitude[0], phase[0], kernel_phase,
      entry_field.reshape(blocks), cotangent[:, 0], tab)
    return (mine * (1.0 / math.sqrt(angles * count)))[:, None]


def solution(mesh):
    return jax.shard_map(
        functools.partial(per_device, mesh.shape["depth"], mesh.shape["illum"]),
        mesh=mesh,
        in_specs=(
            P("depth", "illum", None),
            P("depth", "illum", None),
            P(),
            P(None, "depth", "illum", None, None),
            P(None, "illum", None, None),
        ),
        out_specs=P(None, "depth", "illum", None),
        check_vma=False,
    )
```

```python
import functools
import math

import jax
import jax.numpy as jnp
import ml_dtypes
import numpy as np
from jax import lax
from jax.experimental import pallas as pl
from jax.experimental.pallas import tpu as pltpu
from jax.sharding import PartitionSpec as P

MESH = pl.DeviceIdType.MESH
F32 = jnp.float32
BF16 = jnp.bfloat16


def halves(matrix):
    high = matrix.astype(ml_dtypes.bfloat16)
    low = (matrix - high.astype(np.float64)).astype(ml_dtypes.bfloat16)
    return [high, low]


def tables(length):
    half = length // 2
    lefts = []
    for odd in (0, 1):
        k = 2 * np.arange(half)[:, None] + odd
        angle = (k * np.arange(half)[None, :] % length) * (2.0 * np.pi / length)
        c, s = np.cos(angle), np.sin(angle)
        lefts.append(np.block([[c, s], [-s, c]]))
    lefts += [lefts[0].T, lefts[1].T]
    perm = np.concatenate([np.arange(0, length, 2), np.arange(1, length, 2)])
    shuffle = np.zeros((length, length))
    shuffle[perm, np.arange(length)] = 1.0
    wide, tall = [], []
    for high, low in map(halves, lefts):
        wide.append(np.concatenate([high, high, low], axis=1))
    for high, low in map(halves, lefts):
        tall.append(np.concatenate([high, high, low], axis=0))
    return np.stack(wide), np.stack(tall), shuffle.astype(ml_dtypes.bfloat16)


def sincos(x):
    y = x * 0.5
    z = y * y
    s = 1.0 / math.factorial(13)
    for order in (11, 9, 7, 5, 3, 1):
        s = s * z + (-1.0) ** (order // 2) / math.factorial(order)
    s = s * y
    c = 1.0 / math.factorial(12)
    for order in (10, 8, 6, 4, 2, 0):
        c = c * z + (-1.0) ** (order // 2) / math.factorial(order)
    return 2.0 * s * c, 1.0 - 2.0 * s * s


def split(v):
    high = v.astype(BF16)
    return high, (v - high.astype(F32)).astype(BF16)


def dot(a, b):
    return jnp.dot(a, b, preferred_element_type=F32)


def right(v, tab, at):
    high, low = split(v)
    return dot(jnp.concatenate([high, low, high], axis=1), tab[at])


def left(v, tab, at):
    high, low = split(v)
    return dot(tab[at], jnp.concatenate([high, low, high], axis=0))


def kernel(
    depth, count, amp_hbm, phase_hbm, kern_hbm, psi_hbm, cot_hbm, wide_hbm, tall_hbm, shuffle_hbm, out_ref,
    amp_ref, phase_ref, kern_ref, psi_ref, wide, tall, shuffle_ref,
    x_ref, h_ref, tmp_ref, own_ref, t_ref, end_ref, give_ref, got_ref, keep_ref, land_ref, loaded,
    z_send, z_recv, g_send, g_recv, c_send, c_recv, twin_send, twin_recv, r_send, r_recv,
):
    length = kern_ref.shape[0]
    half = length // 2
    rows = amp_ref.shape[0]
    chips = count // 2
    d = lax.axis_index("depth")
    me = lax.axis_index("illum")
    chip, core = me // 2, me % 2
    needed = depth - 1 - d

    loads = [
        pltpu.make_async_copy(source, target, loaded.at[i])
        for i, (source, target) in enumerate([
            (amp_hbm, amp_ref), (phase_hbm, phase_ref), (kern_hbm, kern_ref),
            (shuffle_hbm, shuffle_ref), (cot_hbm, x_ref), (tall_hbm, tall),
            (wide_hbm, wide), (psi_hbm, psi_ref)])
    ]
    for load in loads:
        load.start()

    def near(p):
        return (chip + p) % chips

    def owner(p):
        if p < chips:
            return 2 * near(p) + core
        return 2 * near(p - chips) + 1 - core

    def rows_of(p):
        return pl.ds(pl.multiple_of(owner(p) * rows, rows), rows)

    twin = (d, 2 * chip + 1 - core)
    barrier = pltpu.get_barrier_semaphore()
    for o in range(1, depth):
        pl.semaphore_signal(barrier, inc=1, device_id=((d + o) % depth, me), device_id_type=MESH)
    for p in range(1, chips + 1):
        peer = (d, owner(p)) if p < chips else twin
        pl.semaphore_signal(barrier, inc=1, device_id=peer, device_id_type=MESH)

    loads[0].wait()
    loads[1].wait()
    sin_t, cos_t = sincos(phase_ref[...])
    own_ref[0] = amp_ref[...] * cos_t
    own_ref[1] = amp_ref[...] * sin_t

    pl.semaphore_wait(barrier, depth - 1 + chips)

    def z_copy(target):
        return pltpu.make_async_remote_copy(
            src_ref=own_ref, dst_ref=t_ref.at[needed, 0],
            send_sem=z_send.at[target], recv_sem=z_recv.at[needed],
            device_id=(target, me), device_id_type=MESH,
        )

    def post(g):
        target = g + 1 - needed

        @pl.when(jnp.logical_and(target >= 0, target < d))
        def _():
            z_copy(target).start()

    post(-1)

    def g_copy(s, p):
        return pltpu.make_async_remote_copy(
            src_ref=t_ref.at[s, 0], dst_ref=t_ref.at[s, chips - p],
            send_sem=g_send.at[s, p], recv_sem=g_recv.at[s, chips - p],
            device_id=(d, owner(p)), device_id_type=MESH,
        )

    def c_copy(s, first, size):
        which = min(first, 1)
        return pltpu.make_async_remote_copy(
            src_ref=t_ref.at[s, pl.ds(first, size)],
            dst_ref=t_ref.at[s, pl.ds(chips + first, size)],
            send_sem=c_send.at[s, which], recv_sem=c_recv.at[s, which],
            device_id=twin, device_id_type=MESH,
        )

    def advance(s, step):
        @pl.when(s < needed)
        def _():
            if step == 0:
                pltpu.make_async_copy(own_ref, t_ref.at[s, 0], z_recv.at[s]).wait()
                for p in range(1, chips):
                    g_copy(s, p).start()
                c_copy(s, 0, 1).start()
            elif step == 1:
                for p in range(1, chips):
                    pltpu.make_async_copy(own_ref, t_ref.at[s, p], g_recv.at[s, p]).wait()
                if chips > 1:
                    c_copy(s, 1, chips - 1).start()
            else:
                c_copy(s, 0, 1).wait_recv()
                if chips > 1:
                    c_copy(s, 1, chips - 1).wait_recv()

    loads[2].wait()
    loads[3].wait()
    phase = kern_ref[...]
    first, rest = split(phase)
    rest = phase - first.astype(F32)
    second, third = split(rest)
    shuffle = shuffle_ref[...]
    moved = (dot(third, shuffle) + dot(second, shuffle)) + dot(first, shuffle)
    tmp_ref[0], tmp_ref[1] = moved[:, :half], moved[:, half:]
    scale = 1.0 / (length * length)
    for odd in (0, 1):
        for c in (0, 1):
            sin_h, cos_h = sincos(tmp_ref[c, pl.ds(odd, half, stride=2), :])
            at = (pl.ds(odd * half, half), pl.ds(c * half, half))
            h_ref[(0, *at)] = cos_h * scale
            h_ref[(1, *at)] = sin_h * scale

    for load in loads[4:7]:
        load.wait()

    def propagate(slot):
        re, im = x_ref[0], x_ref[1]
        parts = []
        for sign, at in ((1, 2), (-1, 3)):
            mixed = jnp.concatenate(
                [v[:, :half] + sign * v[:, half:] for v in (re, im)], axis=1)
            parts.append(right(mixed, tall, at))
        slot(0)
        even, odd = parts
        back = []
        mixes = []
        for sign, at in ((1, 0), (-1, 1)):
            stack = jnp.concatenate([
                jnp.concatenate([
                    v[:half, c * half:(c + 1) * half] + sign * v[half:, c * half:(c + 1) * half]
                    for v in (even, odd)], axis=1)
                for c in (0, 1)], axis=0)
            freq = left(stack, wide, at)
            f_re, f_im = freq[:half], freq[half:]
            h_re = h_ref[0, at * half:(at + 1) * half]
            h_im = h_ref[1, at * half:(at + 1) * half]
            mixes.append(jnp.concatenate(
                [f_re * h_re + f_im * h_im, f_im * h_re - f_re * h_im], axis=0))
        slot(1)
        for at in (0, 1):
            back.append(left(mixes[at], wide, 2 + at))
        slot(2)
        e, o = back
        total, gap = e + o, e - o
        ends = []
        for c in (0, 1):
            cols = slice(c * half, (c + 1) * half)
            mixed = jnp.concatenate([
                jnp.concatenate([total[:half, cols], gap[:half, cols]], axis=0),
                jnp.concatenate([total[half:, cols], gap[half:, cols]], axis=0)], axis=1)
            ends.append(mixed)
        return ends

    def finish(ends):
        e, o = [right(v, tall, at) for at, v in enumerate(ends)]
        total, gap = e + o, e - o
        return (
            jnp.concatenate([total[:, :half], gap[:, :half]], axis=1),
            jnp.concatenate([total[:, half:], gap[:, half:]], axis=1),
        )

    def slot(q, k):
        post(q * 4 + k)
        if k == 0:
            @pl.when(q == 0)
            def _():
                advance(q, 0)
        elif k == 1:
            advance(q, 1)
            advance(q + 1, 0)
        elif k == 3:
            advance(q, 2)

    def body(q, carry):
        x_ref[0], x_ref[1] = finish(propagate(functools.partial(slot, q)))
        slot(q, 3)
        for p in range(count):
            at = rows_of(p)
            t_re, t_im = t_ref[q, p, 0], t_ref[q, p, 1]
            u_re, u_im = x_ref[0, at], x_ref[1, at]
            x_ref[0, at] = u_re * t_re + u_im * t_im
            x_ref[1, at] = u_im * t_re - u_re * t_im
        return carry

    lax.fori_loop(0, needed, body, 0)
    ends = propagate(lambda k: post(needed * 4 + k))
    for c in (0, 1):
        end_ref[c] = ends[c].reshape(chips, 2, rows, length)

    @pl.loop(jnp.minimum(needed * 4 + 4 - needed, d), d)
    def _(target):
        z_copy(target).start()

    def products(to_ref, kind):
        flat = (chips * rows, length)
        u_re, u_im = finish([end_ref[c, :, kind].reshape(flat) for c in (0, 1)])
        p_re, p_im = [psi_ref[c, :, kind].reshape(flat) for c in (0, 1)]
        shape = (chips, rows, length)
        to_ref[:, 0] = (u_re * p_re + u_im * p_im).reshape(shape)
        to_ref[:, 1] = (u_im * p_re - u_re * p_im).reshape(shape)

    def twin_copy(p):
        at = near(p)
        return pltpu.make_async_remote_copy(
            src_ref=give_ref.at[at], dst_ref=got_ref.at[at],
            send_sem=twin_send.at[p], recv_sem=twin_recv.at[p],
            device_id=twin, device_id_type=MESH,
        )

    def sum_copy(p):
        return pltpu.make_async_remote_copy(
            src_ref=keep_ref.at[near(p)], dst_ref=land_ref.at[chips - p],
            send_sem=r_send.at[p], recv_sem=r_recv.at[chips - p],
            device_id=(d, owner(p)), device_id_type=MESH,
        )

    loads[7].wait()
    products(give_ref, 1 - core)
    order = [*range(1, chips), 0]
    for p in order:
        twin_copy(p).start()
    products(keep_ref, core)
    for p in order:
        twin_copy(p).wait_recv()
        if p:
            keep_ref[near(p)] += got_ref[near(p)]
            sum_copy(p).start()
    total = keep_ref[chip] + got_ref[chip]
    for p in range(1, chips):
        pltpu.make_async_copy(own_ref, land_ref.at[p], r_recv.at[p]).wait()
        total = total + land_ref[p]
    out_ref[...] = total

    for p in range(chips):
        twin_copy(p).wait_send()
        if p:
            sum_copy(p).wait_send()

    @pl.loop(0, needed)
    def _(s):
        for p in range(1, chips):
            g_copy(s, p).wait_send()
        c_copy(s, 0, 1).wait_send()
        if chips > 1:
            c_copy(s, 1, chips - 1).wait_send()

    @pl.loop(0, d)
    def _(target):
        z_copy(target).wait_send()


def per_device(depth, count, amplitude, phase, kernel_phase, entry_field, cotangent):
    _, rows, length = amplitude.shape
    angles = entry_field.shape[2]
    assert angles == 1 and amplitude.shape[0] == 1 and count % 2 == 0
    chips, above = count // 2, max(depth - 1, 1)
    wide, tall, shuffle = map(jnp.asarray, tables(length))
    field = (2, length, length)
    blocks = (2, chips, 2, rows, length)
    half_sum = (chips, 2, rows, length)
    dma = pltpu.SemaphoreType.DMA
    mine = pl.pallas_call(
        functools.partial(kernel, depth, count),
        out_shape=jax.ShapeDtypeStruct((2, rows, length), F32),
        in_specs=[pl.BlockSpec(memory_space=pltpu.HBM)] * 8,
        out_specs=pl.BlockSpec(memory_space=pltpu.VMEM),
        scratch_shapes=[
            pltpu.VMEM((rows, length), F32),
            pltpu.VMEM((rows, length), F32),
            pltpu.VMEM((length, length), F32),
            pltpu.VMEM(blocks, F32),
            pltpu.VMEM(wide.shape, BF16),
            pltpu.VMEM(tall.shape, BF16),
            pltpu.VMEM(shuffle.shape, BF16),
            pltpu.VMEM(field, F32),
            pltpu.VMEM(field, F32),
            pltpu.VMEM((2, length, length // 2), F32),
            pltpu.VMEM((2, rows, length), F32),
            pltpu.VMEM((above, count, 2, rows, length), F32),
            pltpu.VMEM(blocks, F32),
            pltpu.VMEM(half_sum, F32),
            pltpu.VMEM(half_sum, F32),
            pltpu.VMEM(half_sum, F32),
            pltpu.VMEM(half_sum, F32),
            dma((8,)),
            dma((above,)), dma((above,)),
            dma((above, chips)), dma((above, chips)),
            dma((above, 2)), dma((above, 2)),
            dma((chips,)), dma((chips,)), dma((chips,)), dma((chips,)),
        ],
        compiler_params=pltpu.CompilerParams(
            collective_id=0, has_side_effects=True, vmem_limit_bytes=60 * 1024 * 1024),
    )(amplitude[0], phase[0], kernel_phase,
      entry_field.reshape(blocks), cotangent[:, 0], wide, tall, shuffle)
    return (mine * (1.0 / math.sqrt(angles * count)))[:, None]


def solution(mesh):
    return jax.shard_map(
        functools.partial(per_device, mesh.shape["depth"], mesh.shape["illum"]),
        mesh=mesh,
        in_specs=(
            P("depth", "illum", None),
            P("depth", "illum", None),
            P(),
            P(None, "depth", "illum", None, None),
            P(None, "illum", None, None),
        ),
        out_specs=P(None, "depth", "illum", None),
        check_vma=False,
    )
```

```python
import functools
import math

import jax
import jax.numpy as jnp
import ml_dtypes
import numpy as np
from jax import lax
from jax.experimental import pallas as pl
from jax.experimental.pallas import tpu as pltpu
from jax.sharding import PartitionSpec as P

MESH = pl.DeviceIdType.MESH
F32 = jnp.float32
BF16 = jnp.bfloat16


def halves(matrix):
    high = matrix.astype(ml_dtypes.bfloat16)
    low = (matrix - high.astype(np.float64)).astype(ml_dtypes.bfloat16)
    return [high, low]


def tables(length):
    half = length // 2
    lefts = []
    for odd in (0, 1):
        k = 2 * np.arange(half)[:, None] + odd
        angle = (k * np.arange(half)[None, :] % length) * (2.0 * np.pi / length)
        c, s = np.cos(angle), np.sin(angle)
        lefts.append(np.block([[c, s], [-s, c]]))
    lefts += [lefts[0].T, lefts[1].T]
    perm = np.concatenate([np.arange(0, length, 2), np.arange(1, length, 2)])
    shuffle = np.zeros((length, length))
    shuffle[perm, np.arange(length)] = 1.0
    wide, tall = [], []
    for high, low in map(halves, lefts):
        wide.append(np.concatenate([high, high, low], axis=1))
    for high, low in map(halves, lefts):
        tall.append(np.concatenate([high, high, low], axis=0))
    return np.stack(wide), np.stack(tall), shuffle.astype(ml_dtypes.bfloat16)


def sincos(x):
    y = x * 0.5
    z = y * y
    s = 1.0 / math.factorial(13)
    for order in (11, 9, 7, 5, 3, 1):
        s = s * z + (-1.0) ** (order // 2) / math.factorial(order)
    s = s * y
    c = 1.0 / math.factorial(12)
    for order in (10, 8, 6, 4, 2, 0):
        c = c * z + (-1.0) ** (order // 2) / math.factorial(order)
    return 2.0 * s * c, 1.0 - 2.0 * s * s


def split(v):
    high = v.astype(BF16)
    return high, (v - high.astype(F32)).astype(BF16)


def dot(a, b):
    return jnp.dot(a, b, preferred_element_type=F32)


def right(v, tab, at):
    high, low = split(v)
    return dot(jnp.concatenate([high, low, high], axis=1), tab[at])


def left(v, tab, at):
    high, low = split(v)
    return dot(tab[at], jnp.concatenate([high, low, high], axis=0))


def kernel(
    depth, count, amp_hbm, phase_hbm, kern_hbm, psi_hbm, cot_hbm, wide_hbm, tall_hbm, shuffle_hbm, out_ref,
    amp_ref, phase_ref, kern_ref, psi_ref, wide, tall, shuffle_ref,
    x_ref, h_ref, tmp_ref, own_ref, t_ref, end_ref, give_ref, got_ref, keep_ref, land_ref, loaded,
    z_send, z_recv, g_send, g_recv, c_send, c_recv, twin_send, twin_recv, r_send, r_recv,
):
    length = kern_ref.shape[0]
    half = length // 2
    rows = amp_ref.shape[0]
    chips = count // 2
    d = lax.axis_index("depth")
    me = lax.axis_index("illum")
    chip, core = me // 2, me % 2
    needed = depth - 1 - d

    loads = [
        pltpu.make_async_copy(source, target, loaded.at[i])
        for i, (source, target) in enumerate([
            (amp_hbm, amp_ref), (phase_hbm, phase_ref), (kern_hbm, kern_ref),
            (shuffle_hbm, shuffle_ref), (cot_hbm, x_ref), (tall_hbm, tall),
            (wide_hbm, wide), (psi_hbm, psi_ref)])
    ]
    for load in loads:
        load.start()

    def near(p):
        return (chip + p) % chips

    def owner(p):
        if p < chips:
            return 2 * near(p) + core
        return 2 * near(p - chips) + 1 - core

    twin = (d, 2 * chip + 1 - core)
    barrier = pltpu.get_barrier_semaphore()
    for o in range(1, depth):
        pl.semaphore_signal(barrier, inc=1, device_id=((d + o) % depth, me), device_id_type=MESH)
    for p in range(1, chips + 1):
        peer = (d, owner(p)) if p < chips else twin
        pl.semaphore_signal(barrier, inc=1, device_id=peer, device_id_type=MESH)

    loads[0].wait()
    loads[1].wait()
    sin_t, cos_t = sincos(phase_ref[...])
    own_ref[0] = amp_ref[...] * cos_t
    own_ref[1] = amp_ref[...] * sin_t

    pl.semaphore_wait(barrier, depth - 1 + chips)

    def z_copy(target):
        return pltpu.make_async_remote_copy(
            src_ref=own_ref, dst_ref=t_ref.at[needed, chip, core],
            send_sem=z_send.at[target], recv_sem=z_recv.at[needed],
            device_id=(target, me), device_id_type=MESH,
        )

    def post(g):
        target = g + 1 - needed

        @pl.when(jnp.logical_and(target >= 0, target < d))
        def _():
            z_copy(target).start()

    post(-1)

    def g_copy(s, p):
        return pltpu.make_async_remote_copy(
            src_ref=t_ref.at[s, chip, core], dst_ref=t_ref.at[s, chip, core],
            send_sem=g_send.at[s, p], recv_sem=g_recv.at[s, chips - p],
            device_id=(d, owner(p)), device_id_type=MESH,
        )

    def c_copy(s, p):
        block = t_ref.at[s, near(p), core]
        return pltpu.make_async_remote_copy(
            src_ref=block, dst_ref=block,
            send_sem=c_send.at[s, p], recv_sem=c_recv.at[s, p],
            device_id=twin, device_id_type=MESH,
        )

    def landed(s, p, sem):
        pltpu.make_async_copy(own_ref, t_ref.at[s, near(p), core], sem).wait()

    def spread(s):
        @pl.when(s < needed)
        def _():
            landed(s, 0, z_recv.at[s])
            for p in range(1, chips):
                g_copy(s, p).start()
            c_copy(s, 0).start()

    def pass_on(s):
        @pl.when(s < needed)
        def _():
            for p in range(1, chips):
                landed(s, p, g_recv.at[s, p])
                c_copy(s, p).start()

    def arrived(s):
        for p in range(chips):
            c_copy(s, p).wait_recv()

    loads[2].wait()
    loads[3].wait()
    phase = kern_ref[...]
    first, rest = split(phase)
    rest = phase - first.astype(F32)
    second, third = split(rest)
    shuffle = shuffle_ref[...]
    moved = (dot(third, shuffle) + dot(second, shuffle)) + dot(first, shuffle)
    tmp_ref[0], tmp_ref[1] = moved[:, :half], moved[:, half:]
    scale = 1.0 / (length * length)
    for odd in (0, 1):
        for c in (0, 1):
            sin_h, cos_h = sincos(tmp_ref[c, pl.ds(odd, half, stride=2), :])
            at = (pl.ds(odd * half, half), pl.ds(c * half, half))
            h_ref[(0, *at)] = cos_h * scale
            h_ref[(1, *at)] = sin_h * scale

    for load in loads[4:7]:
        load.wait()

    def propagate(re, im, slot):
        parts = []
        for sign, at in ((1, 2), (-1, 3)):
            mixed = jnp.concatenate(
                [v[:, :half] + sign * v[:, half:] for v in (re, im)], axis=1)
            parts.append(right(mixed, tall, at))
        slot(0)
        even, odd = parts
        back = []
        mixes = []
        for sign, at in ((1, 0), (-1, 1)):
            stack = jnp.concatenate([
                jnp.concatenate([
                    v[:half, c * half:(c + 1) * half] + sign * v[half:, c * half:(c + 1) * half]
                    for v in (even, odd)], axis=1)
                for c in (0, 1)], axis=0)
            freq = left(stack, wide, at)
            f_re, f_im = freq[:half], freq[half:]
            h_re = h_ref[0, at * half:(at + 1) * half]
            h_im = h_ref[1, at * half:(at + 1) * half]
            mixes.append(jnp.concatenate(
                [f_re * h_re + f_im * h_im, f_im * h_re - f_re * h_im], axis=0))
        slot(1)
        for at in (0, 1):
            back.append(left(mixes[at], wide, 2 + at))
        slot(2)
        e, o = back
        total, gap = e + o, e - o
        for c in (0, 1):
            cols = slice(c * half, (c + 1) * half)
            mixed = jnp.concatenate([
                jnp.concatenate([total[:half, cols], gap[:half, cols]], axis=0),
                jnp.concatenate([total[half:, cols], gap[half:, cols]], axis=0)], axis=1)
            end_ref[c] = mixed.reshape(chips, 2, rows, length)

    def finish(ends):
        e, o = [right(v, tall, at) for at, v in enumerate(ends)]
        total, gap = e + o, e - o
        return (
            jnp.concatenate([total[:, :half], gap[:, :half]], axis=1),
            jnp.concatenate([total[:, half:], gap[:, half:]], axis=1),
        )

    def first_slot(k):
        post(k)
        if k == 0:
            spread(0)
        elif k == 1:
            pass_on(0)
            spread(1)

    propagate(x_ref[0], x_ref[1], first_slot)

    @pl.loop(jnp.clip(4 - needed, 0, d), d)
    def _(target):
        z_copy(target).start()

    def body(q, carry):
        def slot(k):
            if k == 1:
                pass_on(q + 1)
                spread(q + 2)

        u_re, u_im = finish([end_ref[c].reshape(length, length) for c in (0, 1)])
        arrived(q)
        t_re, t_im = [t_ref[q, :, :, c].reshape(length, length) for c in (0, 1)]
        propagate(u_re * t_re + u_im * t_im, u_im * t_re - u_re * t_im, slot)
        return carry

    lax.fori_loop(0, needed, body, 0)

    def products(to_ref, kind):
        flat = (chips * rows, length)
        u_re, u_im = finish([end_ref[c, :, kind].reshape(flat) for c in (0, 1)])
        p_re, p_im = [psi_ref[c, :, kind].reshape(flat) for c in (0, 1)]
        shape = (chips, rows, length)
        to_ref[:, 0] = (u_re * p_re + u_im * p_im).reshape(shape)
        to_ref[:, 1] = (u_im * p_re - u_re * p_im).reshape(shape)

    def twin_copy(p):
        at = near(p)
        return pltpu.make_async_remote_copy(
            src_ref=give_ref.at[at], dst_ref=got_ref.at[at],
            send_sem=twin_send.at[p], recv_sem=twin_recv.at[p],
            device_id=twin, device_id_type=MESH,
        )

    def sum_copy(p):
        return pltpu.make_async_remote_copy(
            src_ref=keep_ref.at[near(p)], dst_ref=land_ref.at[chips - p],
            send_sem=r_send.at[p], recv_sem=r_recv.at[chips - p],
            device_id=(d, owner(p)), device_id_type=MESH,
        )

    loads[7].wait()
    products(give_ref, 1 - core)
    order = [*range(1, chips), 0]
    for p in order:
        twin_copy(p).start()
    products(keep_ref, core)
    for p in order:
        twin_copy(p).wait_recv()
        if p:
            keep_ref[near(p)] += got_ref[near(p)]
            sum_copy(p).start()
    total = keep_ref[chip] + got_ref[chip]
    for p in range(1, chips):
        pltpu.make_async_copy(own_ref, land_ref.at[p], r_recv.at[p]).wait()
        total = total + land_ref[p]
    out_ref[...] = total

    for p in range(chips):
        twin_copy(p).wait_send()
        if p:
            sum_copy(p).wait_send()

    @pl.loop(0, needed)
    def _(s):
        for p in range(chips):
            c_copy(s, p).wait_send()
            if p:
                g_copy(s, p).wait_send()

    @pl.loop(0, d)
    def _(target):
        z_copy(target).wait_send()


def per_device(depth, count, amplitude, phase, kernel_phase, entry_field, cotangent):
    _, rows, length = amplitude.shape
    angles = entry_field.shape[2]
    assert angles == 1 and amplitude.shape[0] == 1 and count % 2 == 0
    chips, above = count // 2, max(depth - 1, 1)
    wide, tall, shuffle = map(jnp.asarray, tables(length))
    field = (2, length, length)
    blocks = (2, chips, 2, rows, length)
    half_sum = (chips, 2, rows, length)
    dma = pltpu.SemaphoreType.DMA
    mine = pl.pallas_call(
        functools.partial(kernel, depth, count),
        out_shape=jax.ShapeDtypeStruct((2, rows, length), F32),
        in_specs=[pl.BlockSpec(memory_space=pltpu.HBM)] * 8,
        out_specs=pl.BlockSpec(memory_space=pltpu.VMEM),
        scratch_shapes=[
            pltpu.VMEM((rows, length), F32),
            pltpu.VMEM((rows, length), F32),
            pltpu.VMEM((length, length), F32),
            pltpu.VMEM(blocks, F32),
            pltpu.VMEM(wide.shape, BF16),
            pltpu.VMEM(tall.shape, BF16),
            pltpu.VMEM(shuffle.shape, BF16),
            pltpu.VMEM(field, F32),
            pltpu.VMEM(field, F32),
            pltpu.VMEM((2, length, length // 2), F32),
            pltpu.VMEM((2, rows, length), F32),
            pltpu.VMEM((above, chips, 2, 2, rows, length), F32),
            pltpu.VMEM(blocks, F32),
            pltpu.VMEM(half_sum, F32),
            pltpu.VMEM(half_sum, F32),
            pltpu.VMEM(half_sum, F32),
            pltpu.VMEM(half_sum, F32),
            dma((8,)),
            dma((above,)), dma((above,)),
            dma((above, chips)), dma((above, chips)),
            dma((above, chips)), dma((above, chips)),
            dma((chips,)), dma((chips,)), dma((chips,)), dma((chips,)),
        ],
        compiler_params=pltpu.CompilerParams(
            collective_id=0, has_side_effects=True, vmem_limit_bytes=60 * 1024 * 1024),
    )(amplitude[0], phase[0], kernel_phase,
      entry_field.reshape(blocks), cotangent[:, 0], wide, tall, shuffle)
    return (mine * (1.0 / math.sqrt(angles * count)))[:, None]


def solution(mesh):
    return jax.shard_map(
        functools.partial(per_device, mesh.shape["depth"], mesh.shape["illum"]),
        mesh=mesh,
        in_specs=(
            P("depth", "illum", None),
            P("depth", "illum", None),
            P(),
            P(None, "depth", "illum", None, None),
            P(None, "illum", None, None),
        ),
        out_specs=P(None, "depth", "illum", None),
        check_vma=False,
    )
```

```python
import functools
import math

import jax
import jax.numpy as jnp
import ml_dtypes
import numpy as np
from jax import lax
from jax.experimental import pallas as pl
from jax.experimental.pallas import tpu as pltpu
from jax.sharding import PartitionSpec as P

MESH = pl.DeviceIdType.MESH
F32 = jnp.float32
BF16 = jnp.bfloat16


def halves(matrix):
    high = matrix.astype(ml_dtypes.bfloat16)
    low = (matrix - high.astype(np.float64)).astype(ml_dtypes.bfloat16)
    return [high, low]


def tables(length):
    half = length // 2
    lefts = []
    for odd in (0, 1):
        k = 2 * np.arange(half)[:, None] + odd
        angle = (k * np.arange(half)[None, :] % length) * (2.0 * np.pi / length)
        c, s = np.cos(angle), np.sin(angle)
        lefts.append(np.block([[c, s], [-s, c]]))
    lefts += [lefts[0].T, lefts[1].T]
    perm = np.concatenate([np.arange(0, length, 2), np.arange(1, length, 2)])
    shuffle = np.zeros((length, length))
    shuffle[perm, np.arange(length)] = 1.0
    wide, tall = [], []
    for high, low in map(halves, lefts):
        wide.append(np.concatenate([high, high, low], axis=1))
    for high, low in map(halves, lefts):
        tall.append(np.concatenate([high, high, low], axis=0))
    return np.stack(wide), np.stack(tall), shuffle.astype(ml_dtypes.bfloat16)


def sincos(x):
    y = x * 0.5
    z = y * y
    s = 1.0 / math.factorial(13)
    for order in (11, 9, 7, 5, 3, 1):
        s = s * z + (-1.0) ** (order // 2) / math.factorial(order)
    s = s * y
    c = 1.0 / math.factorial(12)
    for order in (10, 8, 6, 4, 2, 0):
        c = c * z + (-1.0) ** (order // 2) / math.factorial(order)
    return 2.0 * s * c, 1.0 - 2.0 * s * s


def split(v):
    high = v.astype(BF16)
    return high, (v - high.astype(F32)).astype(BF16)


def dot(a, b):
    return jnp.dot(a, b, preferred_element_type=F32)


def right(v, tab, at):
    high, low = split(v)
    return dot(jnp.concatenate([high, low, high], axis=1), tab[at])


def left(v, tab, at):
    high, low = split(v)
    return dot(tab[at], jnp.concatenate([high, low, high], axis=0))


def kernel(
    depth, count, amp_hbm, phase_hbm, kern_hbm, psi_hbm, cot_hbm, wide_hbm, tall_hbm, shuffle_hbm, out_ref,
    amp_ref, phase_ref, kern_ref, psi_ref, wide, tall, shuffle_ref,
    x_ref, h_ref, tmp_ref, own_ref, t_ref, end_ref, give_ref, got_ref, keep_ref, land_ref, loaded,
    z_send, z_recv, g_send, g_recv, c_send, c_recv, twin_send, twin_recv, r_send, r_recv,
):
    length = kern_ref.shape[0]
    half = length // 2
    rows = amp_ref.shape[0]
    chips = count // 2
    d = lax.axis_index("depth")
    me = lax.axis_index("illum")
    chip, core = me // 2, me % 2
    needed = depth - 1 - d

    loads = [
        pltpu.make_async_copy(source, target, loaded.at[i])
        for i, (source, target) in enumerate([
            (amp_hbm, amp_ref), (phase_hbm, phase_ref), (kern_hbm, kern_ref),
            (shuffle_hbm, shuffle_ref), (cot_hbm, x_ref), (tall_hbm, tall),
            (wide_hbm, wide), (psi_hbm, psi_ref)])
    ]
    for load in loads:
        load.start()

    def near(p):
        return (chip + p) % chips

    def owner(p):
        if p < chips:
            return 2 * near(p) + core
        return 2 * near(p - chips) + 1 - core

    twin = (d, 2 * chip + 1 - core)
    barrier = pltpu.get_barrier_semaphore()
    for o in range(1, depth):
        pl.semaphore_signal(barrier, inc=1, device_id=((d + o) % depth, me), device_id_type=MESH)
    for p in range(1, chips + 1):
        peer = (d, owner(p)) if p < chips else twin
        pl.semaphore_signal(barrier, inc=1, device_id=peer, device_id_type=MESH)

    loads[0].wait()
    loads[1].wait()
    sin_t, cos_t = sincos(phase_ref[...])
    own_ref[0] = amp_ref[...] * cos_t
    own_ref[1] = amp_ref[...] * sin_t

    pl.semaphore_wait(barrier, depth - 1 + chips)

    def z_copy(target, c):
        return pltpu.make_async_remote_copy(
            src_ref=own_ref.at[c], dst_ref=t_ref.at[needed, chip, core, c],
            send_sem=z_send.at[target, c], recv_sem=z_recv.at[needed, c],
            device_id=(target, me), device_id_type=MESH,
        )

    def z_start(target):
        z_copy(target, 0).start()
        z_copy(target, 1).start()

    def post(g):
        target = g + 1 - needed

        @pl.when(jnp.logical_and(target >= 0, target < d))
        def _():
            z_start(target)

    post(-1)

    def g_copy(s, p, part=slice(None)):
        block = t_ref.at[s, chip, core, part]
        return pltpu.make_async_remote_copy(
            src_ref=block, dst_ref=block,
            send_sem=g_send.at[s, p], recv_sem=g_recv.at[s, chips - p],
            device_id=(d, owner(p)), device_id_type=MESH,
        )

    def c_copy(s, p):
        block = t_ref.at[s, near(p), core]
        return pltpu.make_async_remote_copy(
            src_ref=block, dst_ref=block,
            send_sem=c_send.at[s, p], recv_sem=c_recv.at[s, p],
            device_id=twin, device_id_type=MESH,
        )

    def spread(s):
        @pl.when(s < needed)
        def _():
            for c in (0, 1):
                pltpu.make_async_copy(
                    own_ref.at[c], t_ref.at[s, chip, core, c], z_recv.at[s, c]).wait()
                for p in range(1, chips):
                    g_copy(s, p, pl.ds(c, 1)).start()
            c_copy(s, 0).start()

    def pass_on(s, p):
        @pl.when(s < needed)
        def _():
            pltpu.make_async_copy(own_ref, t_ref.at[s, near(p), core], g_recv.at[s, p]).wait()
            c_copy(s, p).start()

    def pass_all(s):
        for p in range(1, chips):
            pass_on(s, p)
            if p == 1:
                spread(s + 1)
        if chips == 1:
            spread(s + 1)

    def arrived(s):
        for p in range(chips):
            c_copy(s, p).wait_recv()

    loads[2].wait()
    loads[3].wait()
    phase = kern_ref[...]
    first, rest = split(phase)
    rest = phase - first.astype(F32)
    second, third = split(rest)
    shuffle = shuffle_ref[...]
    moved = (dot(third, shuffle) + dot(second, shuffle)) + dot(first, shuffle)
    tmp_ref[0], tmp_ref[1] = moved[:, :half], moved[:, half:]
    scale = 1.0 / (length * length)
    for odd in (0, 1):
        for c in (0, 1):
            sin_h, cos_h = sincos(tmp_ref[c, pl.ds(odd, half, stride=2), :])
            at = (pl.ds(odd * half, half), pl.ds(c * half, half))
            h_ref[(0, *at)] = cos_h * scale
            h_ref[(1, *at)] = sin_h * scale

    for load in loads[4:7]:
        load.wait()

    def propagate(re, im, slot):
        parts = []
        for sign, at in ((1, 2), (-1, 3)):
            mixed = jnp.concatenate(
                [v[:, :half] + sign * v[:, half:] for v in (re, im)], axis=1)
            parts.append(right(mixed, tall, at))
        slot(0)
        even, odd = parts
        back = []
        mixes = []
        for sign, at in ((1, 0), (-1, 1)):
            stack = jnp.concatenate([
                jnp.concatenate([
                    v[:half, c * half:(c + 1) * half] + sign * v[half:, c * half:(c + 1) * half]
                    for v in (even, odd)], axis=1)
                for c in (0, 1)], axis=0)
            freq = left(stack, wide, at)
            f_re, f_im = freq[:half], freq[half:]
            h_re = h_ref[0, at * half:(at + 1) * half]
            h_im = h_ref[1, at * half:(at + 1) * half]
            mixes.append(jnp.concatenate(
                [f_re * h_re + f_im * h_im, f_im * h_re - f_re * h_im], axis=0))
        slot(1)
        for at in (0, 1):
            back.append(left(mixes[at], wide, 2 + at))
        slot(2)
        e, o = back
        total, gap = e + o, e - o
        for c in (0, 1):
            cols = slice(c * half, (c + 1) * half)
            mixed = jnp.concatenate([
                jnp.concatenate([total[:half, cols], gap[:half, cols]], axis=0),
                jnp.concatenate([total[half:, cols], gap[half:, cols]], axis=0)], axis=1)
            end_ref[c] = mixed.reshape(chips, 2, rows, length)

    def finish(ends):
        e, o = [right(v, tall, at) for at, v in enumerate(ends)]
        total, gap = e + o, e - o
        return (
            jnp.concatenate([total[:, :half], gap[:, :half]], axis=1),
            jnp.concatenate([total[:, half:], gap[:, half:]], axis=1),
        )

    def first_slot(k):
        post(k)
        if k == 0:
            spread(0)
        elif k == 1:
            pass_all(0)

    propagate(x_ref[0], x_ref[1], first_slot)

    @pl.loop(jnp.clip(4 - needed, 0, d), d)
    def _(target):
        z_start(target)

    def body(q, carry):
        def slot(k):
            if k == 1:
                pass_all(q + 1)

        u_re, u_im = finish([end_ref[c].reshape(length, length) for c in (0, 1)])
        arrived(q)
        t_re, t_im = [t_ref[q, :, :, c].reshape(length, length) for c in (0, 1)]
        propagate(u_re * t_re + u_im * t_im, u_im * t_re - u_re * t_im, slot)
        return carry

    lax.fori_loop(0, needed, body, 0)

    def products(to_ref, kind):
        flat = (chips * rows, length)
        u_re, u_im = finish([end_ref[c, :, kind].reshape(flat) for c in (0, 1)])
        p_re, p_im = [psi_ref[c, :, kind].reshape(flat) for c in (0, 1)]
        shape = (chips, rows, length)
        to_ref[:, 0] = (u_re * p_re + u_im * p_im).reshape(shape)
        to_ref[:, 1] = (u_im * p_re - u_re * p_im).reshape(shape)

    def twin_copy(p):
        at = near(p)
        return pltpu.make_async_remote_copy(
            src_ref=give_ref.at[at], dst_ref=got_ref.at[at],
            send_sem=twin_send.at[p], recv_sem=twin_recv.at[p],
            device_id=twin, device_id_type=MESH,
        )

    def sum_copy(p):
        return pltpu.make_async_remote_copy(
            src_ref=keep_ref.at[near(p)], dst_ref=land_ref.at[chips - p],
            send_sem=r_send.at[p], recv_sem=r_recv.at[chips - p],
            device_id=(d, owner(p)), device_id_type=MESH,
        )

    loads[7].wait()
    products(give_ref, 1 - core)
    order = [*range(1, chips), 0]
    for p in order:
        twin_copy(p).start()
    products(keep_ref, core)
    for p in order:
        twin_copy(p).wait_recv()
        if p:
            keep_ref[near(p)] += got_ref[near(p)]
            sum_copy(p).start()
    total = keep_ref[chip] + got_ref[chip]
    for p in range(1, chips):
        pltpu.make_async_copy(own_ref, land_ref.at[p], r_recv.at[p]).wait()
        total = total + land_ref[p]
    out_ref[:, 0] = total * (1.0 / math.sqrt(count))

    for p in range(chips):
        twin_copy(p).wait_send()
        if p:
            sum_copy(p).wait_send()

    @pl.loop(0, needed)
    def _(s):
        for p in range(chips):
            c_copy(s, p).wait_send()
            if p:
                g_copy(s, p).wait_send()

    @pl.loop(0, d)
    def _(target):
        z_copy(target, 0).wait_send()
        z_copy(target, 1).wait_send()


def per_device(depth, count, amplitude, phase, kernel_phase, entry_field, cotangent):
    _, rows, length = amplitude.shape
    angles = entry_field.shape[2]
    assert angles == 1 and amplitude.shape[0] == 1 and count % 2 == 0
    chips, above = count // 2, max(depth - 1, 1)
    wide, tall, shuffle = map(jnp.asarray, tables(length))
    field = (2, length, length)
    blocks = (2, chips, 2, rows, length)
    half_sum = (chips, 2, rows, length)
    dma = pltpu.SemaphoreType.DMA
    return pl.pallas_call(
        functools.partial(kernel, depth, count),
        out_shape=jax.ShapeDtypeStruct((2, 1, rows, length), F32),
        in_specs=[pl.BlockSpec(memory_space=pltpu.HBM)] * 8,
        out_specs=pl.BlockSpec(memory_space=pltpu.VMEM),
        scratch_shapes=[
            pltpu.VMEM((rows, length), F32),
            pltpu.VMEM((rows, length), F32),
            pltpu.VMEM((length, length), F32),
            pltpu.VMEM(blocks, F32),
            pltpu.VMEM(wide.shape, BF16),
            pltpu.VMEM(tall.shape, BF16),
            pltpu.VMEM(shuffle.shape, BF16),
            pltpu.VMEM(field, F32),
            pltpu.VMEM(field, F32),
            pltpu.VMEM((2, length, length // 2), F32),
            pltpu.VMEM((2, rows, length), F32),
            pltpu.VMEM((above, chips, 2, 2, rows, length), F32),
            pltpu.VMEM(blocks, F32),
            pltpu.VMEM(half_sum, F32),
            pltpu.VMEM(half_sum, F32),
            pltpu.VMEM(half_sum, F32),
            pltpu.VMEM(half_sum, F32),
            dma((8,)),
            dma((above, 2)), dma((above, 2)),
            dma((above, chips)), dma((above, chips)),
            dma((above, chips)), dma((above, chips)),
            dma((chips,)), dma((chips,)), dma((chips,)), dma((chips,)),
        ],
        compiler_params=pltpu.CompilerParams(
            collective_id=0, has_side_effects=True, vmem_limit_bytes=60 * 1024 * 1024),
    )(amplitude[0], phase[0], kernel_phase,
      entry_field.reshape(blocks), cotangent[:, 0], wide, tall, shuffle)


def solution(mesh):
    return jax.shard_map(
        functools.partial(per_device, mesh.shape["depth"], mesh.shape["illum"]),
        mesh=mesh,
        in_specs=(
            P("depth", "illum", None),
            P("depth", "illum", None),
            P(),
            P(None, "depth", "illum", None, None),
            P(None, "illum", None, None),
        ),
        out_specs=P(None, "depth", "illum", None),
        check_vma=False,
    )
```

```python
import functools
import math

import jax
import jax.numpy as jnp
import ml_dtypes
import numpy as np
from jax import lax
from jax.experimental import pallas as pl
from jax.experimental.pallas import tpu as pltpu
from jax.sharding import PartitionSpec as P

MESH = pl.DeviceIdType.MESH
F32 = jnp.float32
BF16 = jnp.bfloat16


def halves(matrix):
    high = matrix.astype(ml_dtypes.bfloat16)
    low = (matrix - high.astype(np.float64)).astype(ml_dtypes.bfloat16)
    return [high, low]


def tables(length):
    half = length // 2
    lefts = []
    for odd in (0, 1):
        k = 2 * np.arange(half)[:, None] + odd
        angle = (k * np.arange(half)[None, :] % length) * (2.0 * np.pi / length)
        c, s = np.cos(angle), np.sin(angle)
        lefts.append(np.block([[c, s], [-s, c]]))
    lefts += [lefts[0].T, lefts[1].T]
    perm = np.concatenate([np.arange(0, length, 2), np.arange(1, length, 2)])
    shuffle = np.zeros((length, length))
    shuffle[perm, np.arange(length)] = 1.0
    wide, tall = [], []
    for high, low in map(halves, lefts):
        wide.append(np.concatenate([high, high, low], axis=1))
    for high, low in map(halves, lefts):
        tall.append(np.concatenate([high, high, low], axis=0))
    return np.stack(wide), np.stack(tall), shuffle.astype(ml_dtypes.bfloat16)


def sincos(x):
    y = x * 0.5
    z = y * y
    s = 1.0 / math.factorial(13)
    for order in (11, 9, 7, 5, 3, 1):
        s = s * z + (-1.0) ** (order // 2) / math.factorial(order)
    s = s * y
    c = 1.0 / math.factorial(12)
    for order in (10, 8, 6, 4, 2, 0):
        c = c * z + (-1.0) ** (order // 2) / math.factorial(order)
    return 2.0 * s * c, 1.0 - 2.0 * s * s


def split(v):
    high = v.astype(BF16)
    return high, (v - high.astype(F32)).astype(BF16)


def dot(a, b):
    return jnp.dot(a, b, preferred_element_type=F32)


def right(v, tab, at):
    high, low = split(v)
    return dot(jnp.concatenate([high, low, high], axis=1), tab[at])


def left(v, tab, at):
    high, low = split(v)
    return dot(tab[at], jnp.concatenate([high, low, high], axis=0))


def kernel(
    depth, count, amp_hbm, phase_hbm, kern_hbm, psi_hbm, cot_hbm, wide_hbm, tall_hbm, shuffle_hbm, out_ref,
    amp_ref, phase_ref, kern_ref, psi_ref, wide, tall, shuffle_ref,
    x_ref, h_ref, tmp_ref, own_ref, t_ref, end_ref, give_ref, got_ref, keep_ref, land_ref, loaded,
    z_send, z_recv, n_send, g_send, g_recv, c_send, c_recv, twin_send, twin_recv, r_send, r_recv,
):
    length = kern_ref.shape[0]
    half = length // 2
    rows = amp_ref.shape[0]
    chips = count // 2
    d = lax.axis_index("depth")
    me = lax.axis_index("illum")
    chip, core = me // 2, me % 2
    needed = depth - 1 - d

    loads = [
        pltpu.make_async_copy(source, target, loaded.at[i])
        for i, (source, target) in enumerate([
            (amp_hbm, amp_ref), (phase_hbm, phase_ref), (kern_hbm, kern_ref),
            (shuffle_hbm, shuffle_ref), (cot_hbm, x_ref), (tall_hbm, tall),
            (wide_hbm, wide), (psi_hbm, psi_ref)])
    ]
    for load in loads:
        load.start()

    def near(p):
        return (chip + p) % chips

    def owner(p):
        if p < chips:
            return 2 * near(p) + core
        return 2 * near(p - chips) + 1 - core

    twin = (d, 2 * chip + 1 - core)
    barrier = pltpu.get_barrier_semaphore()

    def greet(plane, block):
        pl.semaphore_signal(barrier, inc=1, device_id=(plane, block), device_id_type=MESH)

    @pl.loop(d + 1, depth)
    def _(plane):
        greet(plane, me)

    for p in range(1, chips):
        greet(d, owner(p))

        @pl.when(d < depth - 1)
        def _():
            greet(d + 1, owner(p))

    greet(*twin)

    loads[0].wait()
    loads[1].wait()
    sin_t, cos_t = sincos(phase_ref[...])
    own_ref[0] = amp_ref[...] * cos_t
    own_ref[1] = amp_ref[...] * sin_t

    pl.semaphore_wait(barrier, d + (chips - 1) * jnp.minimum(d, 1) + chips)

    def z_copy(target, c):
        return pltpu.make_async_remote_copy(
            src_ref=own_ref.at[c], dst_ref=t_ref.at[needed, chip, core, c],
            send_sem=z_send.at[target, c], recv_sem=z_recv.at[needed, c],
            device_id=(target, me), device_id_type=MESH,
        )

    def next_copy(p):
        return pltpu.make_async_remote_copy(
            src_ref=own_ref, dst_ref=t_ref.at[needed, chip, core],
            send_sem=n_send.at[p], recv_sem=g_recv.at[needed, (chips - p) % chips],
            device_id=(d - 1, owner(p)), device_id_type=MESH,
        )

    def z_start(target):
        @pl.when(target < d - 1)
        def _():
            z_copy(target, 0).start()
            z_copy(target, 1).start()

        @pl.when(target == d - 1)
        def _():
            for p in range(chips):
                next_copy(p).start()

    lead = 1 - jnp.minimum(needed, 1)

    def post(g):
        target = g + lead

        @pl.when(jnp.logical_and(target >= 0, target < d))
        def _():
            z_start(target)

    post(-1)

    def g_copy(s, p, part=slice(None)):
        block = t_ref.at[s, chip, core, part]
        return pltpu.make_async_remote_copy(
            src_ref=block, dst_ref=block,
            send_sem=g_send.at[s, p], recv_sem=g_recv.at[s, chips - p],
            device_id=(d, owner(p)), device_id_type=MESH,
        )

    def c_copy(s, p):
        block = t_ref.at[s, near(p), core]
        return pltpu.make_async_remote_copy(
            src_ref=block, dst_ref=block,
            send_sem=c_send.at[s, p], recv_sem=c_recv.at[s, p],
            device_id=twin, device_id_type=MESH,
        )

    def spread(s):
        @pl.when(s < needed - 1)
        def _():
            for c in (0, 1):
                pltpu.make_async_copy(
                    own_ref.at[c], t_ref.at[s, chip, core, c], z_recv.at[s, c]).wait()
                for p in range(1, chips):
                    g_copy(s, p, pl.ds(c, 1)).start()
            c_copy(s, 0).start()

    def pass_on(s, p):
        @pl.when(s < needed if p else s == needed - 1)
        def _():
            pltpu.make_async_copy(own_ref, t_ref.at[s, near(p), core], g_recv.at[s, p]).wait()
            c_copy(s, p).start()

    def pass_all(s):
        for p in [*range(1, chips), 0]:
            pass_on(s, p)
            if p == min(1, chips - 1):
                spread(s + 1)

    def arrived(s):
        for p in range(chips):
            c_copy(s, p).wait_recv()

    loads[2].wait()
    loads[3].wait()
    phase = kern_ref[...]
    first, rest = split(phase)
    rest = phase - first.astype(F32)
    second, third = split(rest)
    shuffle = shuffle_ref[...]
    moved = (dot(third, shuffle) + dot(second, shuffle)) + dot(first, shuffle)
    tmp_ref[0], tmp_ref[1] = moved[:, :half], moved[:, half:]
    scale = 1.0 / (length * length)
    for odd in (0, 1):
        for c in (0, 1):
            sin_h, cos_h = sincos(tmp_ref[c, pl.ds(odd, half, stride=2), :])
            at = (pl.ds(odd * half, half), pl.ds(c * half, half))
            h_ref[(0, *at)] = cos_h * scale
            h_ref[(1, *at)] = sin_h * scale

    for load in loads[4:7]:
        load.wait()

    def propagate(re, im, slot):
        parts = []
        for sign, at in ((1, 2), (-1, 3)):
            mixed = jnp.concatenate(
                [v[:, :half] + sign * v[:, half:] for v in (re, im)], axis=1)
            parts.append(right(mixed, tall, at))
        slot(0)
        even, odd = parts
        back = []
        mixes = []
        for sign, at in ((1, 0), (-1, 1)):
            stack = jnp.concatenate([
                jnp.concatenate([
                    v[:half, c * half:(c + 1) * half] + sign * v[half:, c * half:(c + 1) * half]
                    for v in (even, odd)], axis=1)
                for c in (0, 1)], axis=0)
            freq = left(stack, wide, at)
            f_re, f_im = freq[:half], freq[half:]
            h_re = h_ref[0, at * half:(at + 1) * half]
            h_im = h_ref[1, at * half:(at + 1) * half]
            mixes.append(jnp.concatenate(
                [f_re * h_re + f_im * h_im, f_im * h_re - f_re * h_im], axis=0))
        slot(1)
        for at in (0, 1):
            back.append(left(mixes[at], wide, 2 + at))
        slot(2)
        e, o = back
        total, gap = e + o, e - o
        for c in (0, 1):
            cols = slice(c * half, (c + 1) * half)
            mixed = jnp.concatenate([
                jnp.concatenate([total[:half, cols], gap[:half, cols]], axis=0),
                jnp.concatenate([total[half:, cols], gap[half:, cols]], axis=0)], axis=1)
            end_ref[c] = mixed.reshape(chips, 2, rows, length)

    def finish(ends):
        e, o = [right(v, tall, at) for at, v in enumerate(ends)]
        total, gap = e + o, e - o
        return (
            jnp.concatenate([total[:, :half], gap[:, :half]], axis=1),
            jnp.concatenate([total[:, half:], gap[:, half:]], axis=1),
        )

    def first_slot(k):
        post(k)
        if k == 0:
            spread(0)
        elif k == 1:
            pass_all(0)

    propagate(x_ref[0], x_ref[1], first_slot)

    @pl.loop(jnp.minimum(3 + lead, d), d)
    def _(target):
        z_start(target)

    def body(q, carry):
        def slot(k):
            if k == 1:
                pass_all(q + 1)

        u_re, u_im = finish([end_ref[c].reshape(length, length) for c in (0, 1)])
        arrived(q)
        t_re, t_im = [t_ref[q, :, :, c].reshape(length, length) for c in (0, 1)]
        propagate(u_re * t_re + u_im * t_im, u_im * t_re - u_re * t_im, slot)
        return carry

    lax.fori_loop(0, needed, body, 0)

    def products(to_ref, kind):
        flat = (chips * rows, length)
        u_re, u_im = finish([end_ref[c, :, kind].reshape(flat) for c in (0, 1)])
        p_re, p_im = [psi_ref[c, :, kind].reshape(flat) for c in (0, 1)]
        shape = (chips, rows, length)
        to_ref[:, 0] = (u_re * p_re + u_im * p_im).reshape(shape)
        to_ref[:, 1] = (u_im * p_re - u_re * p_im).reshape(shape)

    def twin_copy(p):
        at = near(p)
        return pltpu.make_async_remote_copy(
            src_ref=give_ref.at[at], dst_ref=got_ref.at[at],
            send_sem=twin_send.at[p], recv_sem=twin_recv.at[p],
            device_id=twin, device_id_type=MESH,
        )

    def sum_copy(p):
        return pltpu.make_async_remote_copy(
            src_ref=keep_ref.at[near(p)], dst_ref=land_ref.at[chips - p],
            send_sem=r_send.at[p], recv_sem=r_recv.at[chips - p],
            device_id=(d, owner(p)), device_id_type=MESH,
        )

    loads[7].wait()
    products(give_ref, 1 - core)
    order = [*range(1, chips), 0]
    for p in order:
        twin_copy(p).start()
    products(keep_ref, core)
    for p in order:
        twin_copy(p).wait_recv()
        if p:
            keep_ref[near(p)] += got_ref[near(p)]
            sum_copy(p).start()
    total = keep_ref[chip] + got_ref[chip]
    for p in range(1, chips):
        pltpu.make_async_copy(own_ref, land_ref.at[p], r_recv.at[p]).wait()
        total = total + land_ref[p]
    out_ref[:, 0] = total * (1.0 / math.sqrt(count))

    for p in range(chips):
        twin_copy(p).wait_send()
        if p:
            sum_copy(p).wait_send()

    @pl.loop(0, needed)
    def _(s):
        for p in range(chips):
            c_copy(s, p).wait_send()

    @pl.loop(0, jnp.maximum(needed - 1, 0))
    def _(s):
        for p in range(1, chips):
            g_copy(s, p).wait_send()

    @pl.loop(0, jnp.maximum(d - 1, 0))
    def _(target):
        z_copy(target, 0).wait_send()
        z_copy(target, 1).wait_send()

    @pl.when(d > 0)
    def _():
        for p in range(chips):
            next_copy(p).wait_send()


def per_device(depth, count, amplitude, phase, kernel_phase, entry_field, cotangent):
    _, rows, length = amplitude.shape
    angles = entry_field.shape[2]
    assert angles == 1 and amplitude.shape[0] == 1 and count % 2 == 0
    chips, above = count // 2, max(depth - 1, 1)
    wide, tall, shuffle = map(jnp.asarray, tables(length))
    field = (2, length, length)
    blocks = (2, chips, 2, rows, length)
    half_sum = (chips, 2, rows, length)
    dma = pltpu.SemaphoreType.DMA
    return pl.pallas_call(
        functools.partial(kernel, depth, count),
        out_shape=jax.ShapeDtypeStruct((2, 1, rows, length), F32),
        in_specs=[pl.BlockSpec(memory_space=pltpu.HBM)] * 8,
        out_specs=pl.BlockSpec(memory_space=pltpu.VMEM),
        scratch_shapes=[
            pltpu.VMEM((rows, length), F32),
            pltpu.VMEM((rows, length), F32),
            pltpu.VMEM((length, length), F32),
            pltpu.VMEM(blocks, F32),
            pltpu.VMEM(wide.shape, BF16),
            pltpu.VMEM(tall.shape, BF16),
            pltpu.VMEM(shuffle.shape, BF16),
            pltpu.VMEM(field, F32),
            pltpu.VMEM(field, F32),
            pltpu.VMEM((2, length, length // 2), F32),
            pltpu.VMEM((2, rows, length), F32),
            pltpu.VMEM((above, chips, 2, 2, rows, length), F32),
            pltpu.VMEM(blocks, F32),
            pltpu.VMEM(half_sum, F32),
            pltpu.VMEM(half_sum, F32),
            pltpu.VMEM(half_sum, F32),
            pltpu.VMEM(half_sum, F32),
            dma((8,)),
            dma((above, 2)), dma((above, 2)), dma((chips,)),
            dma((above, chips)), dma((above, chips)),
            dma((above, chips)), dma((above, chips)),
            dma((chips,)), dma((chips,)), dma((chips,)), dma((chips,)),
        ],
        compiler_params=pltpu.CompilerParams(
            collective_id=0, has_side_effects=True, vmem_limit_bytes=60 * 1024 * 1024),
    )(amplitude[0], phase[0], kernel_phase,
      entry_field.reshape(blocks), cotangent[:, 0], wide, tall, shuffle)


def solution(mesh):
    return jax.shard_map(
        functools.partial(per_device, mesh.shape["depth"], mesh.shape["illum"]),
        mesh=mesh,
        in_specs=(
            P("depth", "illum", None),
            P("depth", "illum", None),
            P(),
            P(None, "depth", "illum", None, None),
            P(None, "illum", None, None),
        ),
        out_specs=P(None, "depth", "illum", None),
        check_vma=False,
    )
```

```python
import functools
import math

import jax
import jax.numpy as jnp
import ml_dtypes
import numpy as np
from jax import lax
from jax.experimental import pallas as pl
from jax.experimental.pallas import tpu as pltpu
from jax.sharding import PartitionSpec as P

MESH = pl.DeviceIdType.MESH
F32 = jnp.float32
BF16 = jnp.bfloat16


def halves(matrix):
    high = matrix.astype(ml_dtypes.bfloat16)
    low = (matrix - high.astype(np.float64)).astype(ml_dtypes.bfloat16)
    return [high, low]


def tables(length):
    half = length // 2
    lefts = []
    for odd in (0, 1):
        k = 2 * np.arange(half)[:, None] + odd
        angle = (k * np.arange(half)[None, :] % length) * (2.0 * np.pi / length)
        c, s = np.cos(angle), np.sin(angle)
        lefts.append(np.block([[c, s], [-s, c]]))
    lefts += [lefts[0].T, lefts[1].T]
    perm = np.concatenate([np.arange(0, length, 2), np.arange(1, length, 2)])
    shuffle = np.zeros((length, length))
    shuffle[perm, np.arange(length)] = 1.0
    wide, tall = [], []
    for high, low in map(halves, lefts):
        wide.append(np.concatenate([high, high, low], axis=1))
    for high, low in map(halves, lefts):
        tall.append(np.concatenate([high, high, low], axis=0))
    return np.stack(wide), np.stack(tall), shuffle.astype(ml_dtypes.bfloat16)


def sincos(x):
    y = x * 0.5
    z = y * y
    s = 1.0 / math.factorial(13)
    for order in (11, 9, 7, 5, 3, 1):
        s = s * z + (-1.0) ** (order // 2) / math.factorial(order)
    s = s * y
    c = 1.0 / math.factorial(12)
    for order in (10, 8, 6, 4, 2, 0):
        c = c * z + (-1.0) ** (order // 2) / math.factorial(order)
    return 2.0 * s * c, 1.0 - 2.0 * s * s


def split(v):
    high = v.astype(BF16)
    return high, (v - high.astype(F32)).astype(BF16)


def dot(a, b):
    return jnp.dot(a, b, preferred_element_type=F32)


def right(v, tab, at):
    high, low = split(v)
    return dot(jnp.concatenate([high, low, high], axis=1), tab[at])


def left(v, tab, at):
    high, low = split(v)
    return dot(tab[at], jnp.concatenate([high, low, high], axis=0))


def kernel(
    depth, count, amp_hbm, phase_hbm, kern_hbm, psi_hbm, cot_hbm, wide_hbm, tall_hbm, shuffle_hbm, out_ref,
    amp_ref, phase_ref, kern_ref, psi_ref, wide, tall, shuffle_ref,
    x_ref, h_ref, tmp_ref, own_ref, t_ref, end_ref, give_ref, got_ref, keep_ref, land_ref, loaded,
    z_send, z_recv, n_send, f_send, g_send, g_recv, c_send, c_recv, twin_send, twin_recv, r_send, r_recv,
):
    length = kern_ref.shape[0]
    half = length // 2
    rows = amp_ref.shape[0]
    chips = count // 2
    d = lax.axis_index("depth")
    me = lax.axis_index("illum")
    chip, core = me // 2, me % 2
    needed = depth - 1 - d

    loads = [
        pltpu.make_async_copy(source, target, loaded.at[i])
        for i, (source, target) in enumerate([
            (amp_hbm, amp_ref), (phase_hbm, phase_ref), (kern_hbm, kern_ref),
            (shuffle_hbm, shuffle_ref), (cot_hbm, x_ref), (tall_hbm, tall),
            (wide_hbm, wide), (psi_hbm, psi_ref)])
    ]
    for load in loads:
        load.start()

    def near(p):
        return (chip + p) % chips

    def owner(p):
        if p < chips:
            return 2 * near(p) + core
        return 2 * near(p - chips) + 1 - core

    twin = (d, 2 * chip + 1 - core)
    barrier = pltpu.get_barrier_semaphore()

    def greet(plane, block):
        pl.semaphore_signal(barrier, inc=1, device_id=(plane, block), device_id_type=MESH)

    @pl.loop(d + 1, depth)
    def _(plane):
        greet(plane, me)

    for p in range(1, chips):
        greet(d, owner(p))

        @pl.when(d < depth - 1)
        def _():
            greet(d + 1, owner(p))

        if depth >= 3:
            @pl.when(d == 0)
            def _():
                greet(depth - 1, owner(p))

    greet(*twin)

    loads[0].wait()
    loads[1].wait()
    sin_t, cos_t = sincos(phase_ref[...])
    own_ref[0] = amp_ref[...] * cos_t
    own_ref[1] = amp_ref[...] * sin_t

    lead = 1 - jnp.minimum(needed, 1)
    peers = jnp.minimum(d, 1) + (lead if depth >= 3 else 0)
    pl.semaphore_wait(barrier, d + (chips - 1) * peers + chips)

    def z_copy(target, c):
        return pltpu.make_async_remote_copy(
            src_ref=own_ref.at[c], dst_ref=t_ref.at[needed, chip, core, c],
            send_sem=z_send.at[target, c], recv_sem=z_recv.at[needed, c],
            device_id=(target, me), device_id_type=MESH,
        )

    def next_copy(p):
        return pltpu.make_async_remote_copy(
            src_ref=own_ref, dst_ref=t_ref.at[needed, chip, core],
            send_sem=n_send.at[p], recv_sem=g_recv.at[needed, (chips - p) % chips],
            device_id=(d - 1, owner(p)), device_id_type=MESH,
        )

    def far_copy(p):
        return pltpu.make_async_remote_copy(
            src_ref=own_ref.at[1], dst_ref=t_ref.at[0, chip, core, 1],
            send_sem=f_send.at[p], recv_sem=g_recv.at[0, chips - p],
            device_id=(0, owner(p)), device_id_type=MESH,
        )

    def z_start(target):
        @pl.when(target < d - 1)
        def _():
            z_copy(target, 0).start()
            if depth >= 3:
                @pl.when(jnp.logical_and(d == depth - 1, target == 0))
                def _():
                    for p in range(1, chips):
                        far_copy(p).start()
            z_copy(target, 1).start()

        @pl.when(target == d - 1)
        def _():
            for p in range(chips):
                next_copy(p).start()

    def post(g):
        target = g + lead

        @pl.when(jnp.logical_and(target >= 0, target < d))
        def _():
            z_start(target)

    post(-1)

    def g_copy(s, p, part):
        half_at = part.start
        block = t_ref.at[s, chip, core, part]
        return pltpu.make_async_remote_copy(
            src_ref=block, dst_ref=block,
            send_sem=g_send.at[s, p, half_at], recv_sem=g_recv.at[s, chips - p],
            device_id=(d, owner(p)), device_id_type=MESH,
        )

    def c_copy(s, p):
        block = t_ref.at[s, near(p), core]
        return pltpu.make_async_remote_copy(
            src_ref=block, dst_ref=block,
            send_sem=c_send.at[s, p], recv_sem=c_recv.at[s, p],
            device_id=twin, device_id_type=MESH,
        )

    def spread(s):
        @pl.when(s < needed - 1)
        def _():
            for c in (0, 1):
                pltpu.make_async_copy(
                    own_ref.at[c], t_ref.at[s, chip, core, c], z_recv.at[s, c]).wait()

                @pl.when(jnp.logical_or(c == 0, jnp.logical_or(s > 0, d > 0)))
                def _():
                    for p in range(1, chips):
                        g_copy(s, p, pl.ds(c, 1)).start()
            c_copy(s, 0).start()

    def pass_on(s, p):
        @pl.when(s < needed if p else s == needed - 1)
        def _():
            pltpu.make_async_copy(own_ref, t_ref.at[s, near(p), core], g_recv.at[s, p]).wait()
            c_copy(s, p).start()

    def pass_all(s):
        for p in [*range(1, chips), 0]:
            pass_on(s, p)
            if p == min(1, chips - 1):
                spread(s + 1)

    def arrived(s):
        for p in range(chips):
            c_copy(s, p).wait_recv()

    loads[2].wait()
    loads[3].wait()
    phase = kern_ref[...]
    first, rest = split(phase)
    rest = phase - first.astype(F32)
    second, third = split(rest)
    shuffle = shuffle_ref[...]
    moved = (dot(third, shuffle) + dot(second, shuffle)) + dot(first, shuffle)
    tmp_ref[0], tmp_ref[1] = moved[:, :half], moved[:, half:]
    scale = 1.0 / (length * length)
    for odd in (0, 1):
        for c in (0, 1):
            sin_h, cos_h = sincos(tmp_ref[c, pl.ds(odd, half, stride=2), :])
            at = (pl.ds(odd * half, half), pl.ds(c * half, half))
            h_ref[(0, *at)] = cos_h * scale
            h_ref[(1, *at)] = sin_h * scale

    for load in loads[4:7]:
        load.wait()

    def propagate(re, im, slot):
        parts = []
        for sign, at in ((1, 2), (-1, 3)):
            mixed = jnp.concatenate(
                [v[:, :half] + sign * v[:, half:] for v in (re, im)], axis=1)
            parts.append(right(mixed, tall, at))
        slot(0)
        even, odd = parts
        back = []
        mixes = []
        for sign, at in ((1, 0), (-1, 1)):
            stack = jnp.concatenate([
                jnp.concatenate([
                    v[:half, c * half:(c + 1) * half] + sign * v[half:, c * half:(c + 1) * half]
                    for v in (even, odd)], axis=1)
                for c in (0, 1)], axis=0)
            freq = left(stack, wide, at)
            f_re, f_im = freq[:half], freq[half:]
            h_re = h_ref[0, at * half:(at + 1) * half]
            h_im = h_ref[1, at * half:(at + 1) * half]
            mixes.append(jnp.concatenate(
                [f_re * h_re + f_im * h_im, f_im * h_re - f_re * h_im], axis=0))
        slot(1)
        for at in (0, 1):
            back.append(left(mixes[at], wide, 2 + at))
        slot(2)
        e, o = back
        total, gap = e + o, e - o
        for c in (0, 1):
            cols = slice(c * half, (c + 1) * half)
            mixed = jnp.concatenate([
                jnp.concatenate([total[:half, cols], gap[:half, cols]], axis=0),
                jnp.concatenate([total[half:, cols], gap[half:, cols]], axis=0)], axis=1)
            end_ref[c] = mixed.reshape(chips, 2, rows, length)

    def finish(ends):
        e, o = [right(v, tall, at) for at, v in enumerate(ends)]
        total, gap = e + o, e - o
        return (
            jnp.concatenate([total[:, :half], gap[:, :half]], axis=1),
            jnp.concatenate([total[:, half:], gap[:, half:]], axis=1),
        )

    def first_slot(k):
        post(k)
        if k == 0:
            spread(0)
        elif k == 1:
            pass_all(0)

    propagate(x_ref[0], x_ref[1], first_slot)

    @pl.loop(jnp.minimum(3 + lead, d), d)
    def _(target):
        z_start(target)

    def body(q, carry):
        def slot(k):
            if k == 1:
                pass_all(q + 1)

        u_re, u_im = finish([end_ref[c].reshape(length, length) for c in (0, 1)])
        arrived(q)
        t_re, t_im = [t_ref[q, :, :, c].reshape(length, length) for c in (0, 1)]
        propagate(u_re * t_re + u_im * t_im, u_im * t_re - u_re * t_im, slot)
        return carry

    lax.fori_loop(0, needed, body, 0)

    def products(to_ref, kind):
        flat = (chips * rows, length)
        u_re, u_im = finish([end_ref[c, :, kind].reshape(flat) for c in (0, 1)])
        p_re, p_im = [psi_ref[c, :, kind].reshape(flat) for c in (0, 1)]
        shape = (chips, rows, length)
        to_ref[:, 0] = (u_re * p_re + u_im * p_im).reshape(shape)
        to_ref[:, 1] = (u_im * p_re - u_re * p_im).reshape(shape)

    def twin_copy(p):
        at = near(p)
        return pltpu.make_async_remote_copy(
            src_ref=give_ref.at[at], dst_ref=got_ref.at[at],
            send_sem=twin_send.at[p], recv_sem=twin_recv.at[p],
            device_id=twin, device_id_type=MESH,
        )

    def sum_copy(p):
        return pltpu.make_async_remote_copy(
            src_ref=keep_ref.at[near(p)], dst_ref=land_ref.at[chips - p],
            send_sem=r_send.at[p], recv_sem=r_recv.at[chips - p],
            device_id=(d, owner(p)), device_id_type=MESH,
        )

    loads[7].wait()
    products(give_ref, 1 - core)
    order = [*range(1, chips), 0]
    for p in order:
        twin_copy(p).start()
    products(keep_ref, core)
    for p in order:
        twin_copy(p).wait_recv()
        if p:
            keep_ref[near(p)] += got_ref[near(p)]
            sum_copy(p).start()
    total = keep_ref[chip] + got_ref[chip]
    for p in range(1, chips):
        pltpu.make_async_copy(own_ref, land_ref.at[p], r_recv.at[p]).wait()
        total = total + land_ref[p]
    out_ref[:, 0] = total * (1.0 / math.sqrt(count))

    for p in range(chips):
        twin_copy(p).wait_send()
        if p:
            sum_copy(p).wait_send()

    @pl.loop(0, needed)
    def _(s):
        for p in range(chips):
            c_copy(s, p).wait_send()

    @pl.loop(0, jnp.maximum(needed - 1, 0))
    def _(s):
        for p in range(1, chips):
            g_copy(s, p, pl.ds(0, 1)).wait_send()

            @pl.when(jnp.logical_or(s > 0, d > 0))
            def _():
                g_copy(s, p, pl.ds(1, 1)).wait_send()

    @pl.loop(0, jnp.maximum(d - 1, 0))
    def _(target):
        z_copy(target, 0).wait_send()
        z_copy(target, 1).wait_send()

    @pl.when(d > 0)
    def _():
        for p in range(chips):
            next_copy(p).wait_send()

    if depth >= 3:
        @pl.when(d == depth - 1)
        def _():
            for p in range(1, chips):
                far_copy(p).wait_send()


def per_device(depth, count, amplitude, phase, kernel_phase, entry_field, cotangent):
    _, rows, length = amplitude.shape
    angles = entry_field.shape[2]
    assert angles == 1 and amplitude.shape[0] == 1 and count % 2 == 0
    chips, above = count // 2, max(depth - 1, 1)
    wide, tall, shuffle = map(jnp.asarray, tables(length))
    field = (2, length, length)
    blocks = (2, chips, 2, rows, length)
    half_sum = (chips, 2, rows, length)
    dma = pltpu.SemaphoreType.DMA
    return pl.pallas_call(
        functools.partial(kernel, depth, count),
        out_shape=jax.ShapeDtypeStruct((2, 1, rows, length), F32),
        in_specs=[pl.BlockSpec(memory_space=pltpu.HBM)] * 8,
        out_specs=pl.BlockSpec(memory_space=pltpu.VMEM),
        scratch_shapes=[
            pltpu.VMEM((rows, length), F32),
            pltpu.VMEM((rows, length), F32),
            pltpu.VMEM((length, length), F32),
            pltpu.VMEM(blocks, F32),
            pltpu.VMEM(wide.shape, BF16),
            pltpu.VMEM(tall.shape, BF16),
            pltpu.VMEM(shuffle.shape, BF16),
            pltpu.VMEM(field, F32),
            pltpu.VMEM(field, F32),
            pltpu.VMEM((2, length, length // 2), F32),
            pltpu.VMEM((2, rows, length), F32),
            pltpu.VMEM((above, chips, 2, 2, rows, length), F32),
            pltpu.VMEM(blocks, F32),
            pltpu.VMEM(half_sum, F32),
            pltpu.VMEM(half_sum, F32),
            pltpu.VMEM(half_sum, F32),
            pltpu.VMEM(half_sum, F32),
            dma((8,)),
            dma((above, 2)), dma((above, 2)), dma((chips,)), dma((chips,)),
            dma((above, chips, 2)), dma((above, chips)),
            dma((above, chips)), dma((above, chips)),
            dma((chips,)), dma((chips,)), dma((chips,)), dma((chips,)),
        ],
        compiler_params=pltpu.CompilerParams(
            collective_id=0, has_side_effects=True, vmem_limit_bytes=60 * 1024 * 1024),
    )(amplitude[0], phase[0], kernel_phase,
      entry_field.reshape(blocks), cotangent[:, 0], wide, tall, shuffle)


def solution(mesh):
    return jax.shard_map(
        functools.partial(per_device, mesh.shape["depth"], mesh.shape["illum"]),
        mesh=mesh,
        in_specs=(
            P("depth", "illum", None),
            P("depth", "illum", None),
            P(),
            P(None, "depth", "illum", None, None),
            P(None, "illum", None, None),
        ),
        out_specs=P(None, "depth", "illum", None),
        check_vma=False,
    )
```

```python
import functools
import math

import jax
import jax.numpy as jnp
import ml_dtypes
import numpy as np
from jax import lax
from jax.experimental import pallas as pl
from jax.experimental.pallas import tpu as pltpu
from jax.sharding import PartitionSpec as P

MESH = pl.DeviceIdType.MESH
F32 = jnp.float32
BF16 = jnp.bfloat16


def halves(matrix):
    high = matrix.astype(ml_dtypes.bfloat16)
    low = (matrix - high.astype(np.float64)).astype(ml_dtypes.bfloat16)
    return [high, low]


def tables(length):
    half = length // 2
    lefts = []
    for odd in (0, 1):
        k = 2 * np.arange(half)[:, None] + odd
        angle = (k * np.arange(half)[None, :] % length) * (2.0 * np.pi / length)
        c, s = np.cos(angle), np.sin(angle)
        lefts.append(np.block([[c, s], [-s, c]]))
    lefts += [lefts[0].T, lefts[1].T]
    perm = np.concatenate([np.arange(0, length, 2), np.arange(1, length, 2)])
    shuffle = np.zeros((length, length))
    shuffle[perm, np.arange(length)] = 1.0
    wide, tall = [], []
    for high, low in map(halves, lefts):
        wide.append(np.concatenate([high, low], axis=0))
    for high, low in map(halves, lefts):
        tall.append(np.concatenate([high, low], axis=0))
    return np.stack(wide), np.stack(tall), shuffle.astype(ml_dtypes.bfloat16)


def sincos(x):
    y = x * 0.5
    z = y * y
    s = 1.0 / math.factorial(13)
    for order in (11, 9, 7, 5, 3, 1):
        s = s * z + (-1.0) ** (order // 2) / math.factorial(order)
    s = s * y
    c = 1.0 / math.factorial(12)
    for order in (10, 8, 6, 4, 2, 0):
        c = c * z + (-1.0) ** (order // 2) / math.factorial(order)
    return 2.0 * s * c, 1.0 - 2.0 * s * s


def split(v):
    high = v.astype(BF16)
    return high, (v - high.astype(F32)).astype(BF16)


def dot(a, b):
    return jnp.dot(a, b, preferred_element_type=F32)


def right(v, tab, at):
    rows, length = v.shape
    high, low = split(v)
    main = dot(jnp.concatenate([high, low], axis=0), tab[at, :length])
    return main[:rows] + (main[rows:] + dot(high, tab[at, length:]))


def left(v, tab, at):
    length = v.shape[0]
    high, low = split(v)
    main = dot(tab[at], high)
    return main[:length] + (main[length:] + dot(tab[at, :length], low))


def kernel(
    depth, count, amp_hbm, phase_hbm, kern_hbm, psi_hbm, cot_hbm, wide_hbm, tall_hbm, shuffle_hbm, out_ref,
    amp_ref, phase_ref, kern_ref, psi_ref, wide, tall, shuffle_ref,
    x_ref, h_ref, tmp_ref, own_ref, t_ref, end_ref, give_ref, got_ref, keep_ref, land_ref, loaded,
    z_send, z_recv, n_send, f_send, g_send, g_recv, c_send, c_recv, twin_send, twin_recv, r_send, r_recv,
):
    length = kern_ref.shape[0]
    half = length // 2
    rows = amp_ref.shape[0]
    chips = count // 2
    d = lax.axis_index("depth")
    me = lax.axis_index("illum")
    chip, core = me // 2, me % 2
    needed = depth - 1 - d

    loads = [
        pltpu.make_async_copy(source, target, loaded.at[i])
        for i, (source, target) in enumerate([
            (amp_hbm, amp_ref), (phase_hbm, phase_ref), (kern_hbm, kern_ref),
            (shuffle_hbm, shuffle_ref), (cot_hbm, x_ref), (tall_hbm, tall),
            (wide_hbm, wide), (psi_hbm, psi_ref)])
    ]
    for load in loads:
        load.start()

    def near(p):
        return (chip + p) % chips

    def owner(p):
        if p < chips:
            return 2 * near(p) + core
        return 2 * near(p - chips) + 1 - core

    twin = (d, 2 * chip + 1 - core)
    barrier = pltpu.get_barrier_semaphore()

    def greet(plane, block):
        pl.semaphore_signal(barrier, inc=1, device_id=(plane, block), device_id_type=MESH)

    @pl.loop(d + 1, depth)
    def _(plane):
        greet(plane, me)

    for p in range(1, chips):
        greet(d, owner(p))

        @pl.when(d < depth - 1)
        def _():
            greet(d + 1, owner(p))

        if depth >= 3:
            @pl.when(d == 0)
            def _():
                greet(depth - 1, owner(p))

    greet(*twin)

    loads[0].wait()
    loads[1].wait()
    sin_t, cos_t = sincos(phase_ref[...])
    own_ref[0] = amp_ref[...] * cos_t
    own_ref[1] = amp_ref[...] * sin_t

    lead = 1 - jnp.minimum(needed, 1)
    peers = jnp.minimum(d, 1) + (lead if depth >= 3 else 0)
    pl.semaphore_wait(barrier, d + (chips - 1) * peers + chips)

    def z_copy(target, c):
        return pltpu.make_async_remote_copy(
            src_ref=own_ref.at[c], dst_ref=t_ref.at[needed, chip, core, c],
            send_sem=z_send.at[target, c], recv_sem=z_recv.at[needed, c],
            device_id=(target, me), device_id_type=MESH,
        )

    def next_copy(p):
        return pltpu.make_async_remote_copy(
            src_ref=own_ref, dst_ref=t_ref.at[needed, chip, core],
            send_sem=n_send.at[p], recv_sem=g_recv.at[needed, (chips - p) % chips],
            device_id=(d - 1, owner(p)), device_id_type=MESH,
        )

    def far_copy(p):
        return pltpu.make_async_remote_copy(
            src_ref=own_ref.at[1], dst_ref=t_ref.at[0, chip, core, 1],
            send_sem=f_send.at[p], recv_sem=g_recv.at[0, chips - p],
            device_id=(0, owner(p)), device_id_type=MESH,
        )

    def z_start(target):
        @pl.when(target < d - 1)
        def _():
            z_copy(target, 0).start()
            if depth >= 3:
                @pl.when(jnp.logical_and(d == depth - 1, target == 0))
                def _():
                    for p in range(1, chips):
                        far_copy(p).start()
            z_copy(target, 1).start()

        @pl.when(target == d - 1)
        def _():
            for p in range(chips):
                next_copy(p).start()

    def post(g):
        target = g + lead

        @pl.when(jnp.logical_and(target >= 0, target < d))
        def _():
            z_start(target)

    post(-1)

    def g_copy(s, p, part):
        half_at = part.start
        block = t_ref.at[s, chip, core, part]
        return pltpu.make_async_remote_copy(
            src_ref=block, dst_ref=block,
            send_sem=g_send.at[s, p, half_at], recv_sem=g_recv.at[s, chips - p],
            device_id=(d, owner(p)), device_id_type=MESH,
        )

    def c_copy(s, p):
        block = t_ref.at[s, near(p), core]
        return pltpu.make_async_remote_copy(
            src_ref=block, dst_ref=block,
            send_sem=c_send.at[s, p], recv_sem=c_recv.at[s, p],
            device_id=twin, device_id_type=MESH,
        )

    def spread(s):
        @pl.when(s < needed - 1)
        def _():
            for c in (0, 1):
                pltpu.make_async_copy(
                    own_ref.at[c], t_ref.at[s, chip, core, c], z_recv.at[s, c]).wait()

                @pl.when(jnp.logical_or(c == 0, jnp.logical_or(s > 0, d > 0)))
                def _():
                    for p in range(1, chips):
                        g_copy(s, p, pl.ds(c, 1)).start()
            c_copy(s, 0).start()

    def pass_on(s, p):
        @pl.when(s < needed if p else s == needed - 1)
        def _():
            pltpu.make_async_copy(own_ref, t_ref.at[s, near(p), core], g_recv.at[s, p]).wait()
            c_copy(s, p).start()

    def pass_all(s):
        for p in [*range(1, chips), 0]:
            pass_on(s, p)
            if p == min(1, chips - 1):
                spread(s + 1)

    def arrived(s):
        for p in range(chips):
            c_copy(s, p).wait_recv()

    loads[2].wait()
    loads[3].wait()
    phase = kern_ref[...]
    first, rest = split(phase)
    rest = phase - first.astype(F32)
    second, third = split(rest)
    shuffle = shuffle_ref[...]
    moved = (dot(third, shuffle) + dot(second, shuffle)) + dot(first, shuffle)
    tmp_ref[0], tmp_ref[1] = moved[:, :half], moved[:, half:]
    scale = 1.0 / (length * length)
    for odd in (0, 1):
        for c in (0, 1):
            sin_h, cos_h = sincos(tmp_ref[c, pl.ds(odd, half, stride=2), :])
            at = (pl.ds(odd * half, half), pl.ds(c * half, half))
            h_ref[(0, *at)] = cos_h * scale
            h_ref[(1, *at)] = sin_h * scale

    for load in loads[4:7]:
        load.wait()

    def propagate(re, im, slot):
        parts = []
        for sign, at in ((1, 2), (-1, 3)):
            mixed = jnp.concatenate(
                [v[:, :half] + sign * v[:, half:] for v in (re, im)], axis=1)
            parts.append(right(mixed, tall, at))
        slot(0)
        even, odd = parts
        back = []
        mixes = []
        for sign, at in ((1, 0), (-1, 1)):
            stack = jnp.concatenate([
                jnp.concatenate([
                    v[:half, c * half:(c + 1) * half] + sign * v[half:, c * half:(c + 1) * half]
                    for v in (even, odd)], axis=1)
                for c in (0, 1)], axis=0)
            freq = left(stack, wide, at)
            f_re, f_im = freq[:half], freq[half:]
            h_re = h_ref[0, at * half:(at + 1) * half]
            h_im = h_ref[1, at * half:(at + 1) * half]
            mixes.append(jnp.concatenate(
                [f_re * h_re + f_im * h_im, f_im * h_re - f_re * h_im], axis=0))
        slot(1)
        for at in (0, 1):
            back.append(left(mixes[at], wide, 2 + at))
        slot(2)
        e, o = back
        total, gap = e + o, e - o
        for c in (0, 1):
            cols = slice(c * half, (c + 1) * half)
            mixed = jnp.concatenate([
                jnp.concatenate([total[:half, cols], gap[:half, cols]], axis=0),
                jnp.concatenate([total[half:, cols], gap[half:, cols]], axis=0)], axis=1)
            end_ref[c] = mixed.reshape(chips, 2, rows, length)

    def finish(ends):
        e, o = [right(v, tall, at) for at, v in enumerate(ends)]
        total, gap = e + o, e - o
        return (
            jnp.concatenate([total[:, :half], gap[:, :half]], axis=1),
            jnp.concatenate([total[:, half:], gap[:, half:]], axis=1),
        )

    def first_slot(k):
        post(k)
        if k == 0:
            spread(0)
        elif k == 1:
            pass_all(0)

    propagate(x_ref[0], x_ref[1], first_slot)

    @pl.loop(jnp.minimum(3 + lead, d), d)
    def _(target):
        z_start(target)

    def body(q, carry):
        def slot(k):
            if k == 1:
                pass_all(q + 1)

        u_re, u_im = finish([end_ref[c].reshape(length, length) for c in (0, 1)])
        arrived(q)
        t_re, t_im = [t_ref[q, :, :, c].reshape(length, length) for c in (0, 1)]
        propagate(u_re * t_re + u_im * t_im, u_im * t_re - u_re * t_im, slot)
        return carry

    lax.fori_loop(0, needed, body, 0)

    def products(to_ref, kind):
        flat = (chips * rows, length)
        u_re, u_im = finish([end_ref[c, :, kind].reshape(flat) for c in (0, 1)])
        p_re, p_im = [psi_ref[c, :, kind].reshape(flat) for c in (0, 1)]
        shape = (chips, rows, length)
        to_ref[:, 0] = (u_re * p_re + u_im * p_im).reshape(shape)
        to_ref[:, 1] = (u_im * p_re - u_re * p_im).reshape(shape)

    def twin_copy(p):
        at = near(p)
        return pltpu.make_async_remote_copy(
            src_ref=give_ref.at[at], dst_ref=got_ref.at[at],
            send_sem=twin_send.at[p], recv_sem=twin_recv.at[p],
            device_id=twin, device_id_type=MESH,
        )

    def sum_copy(p):
        return pltpu.make_async_remote_copy(
            src_ref=keep_ref.at[near(p)], dst_ref=land_ref.at[chips - p],
            send_sem=r_send.at[p], recv_sem=r_recv.at[chips - p],
            device_id=(d, owner(p)), device_id_type=MESH,
        )

    loads[7].wait()
    products(give_ref, 1 - core)
    order = [*range(1, chips), 0]
    for p in order:
        twin_copy(p).start()
    products(keep_ref, core)
    for p in order:
        twin_copy(p).wait_recv()
        if p:
            keep_ref[near(p)] += got_ref[near(p)]
            sum_copy(p).start()
    total = keep_ref[chip] + got_ref[chip]
    for p in range(1, chips):
        pltpu.make_async_copy(own_ref, land_ref.at[p], r_recv.at[p]).wait()
        total = total + land_ref[p]
    out_ref[:, 0] = total * (1.0 / math.sqrt(count))

    for p in range(chips):
        twin_copy(p).wait_send()
        if p:
            sum_copy(p).wait_send()

    @pl.loop(0, needed)
    def _(s):
        for p in range(chips):
            c_copy(s, p).wait_send()

    @pl.loop(0, jnp.maximum(needed - 1, 0))
    def _(s):
        for p in range(1, chips):
            g_copy(s, p, pl.ds(0, 1)).wait_send()

            @pl.when(jnp.logical_or(s > 0, d > 0))
            def _():
                g_copy(s, p, pl.ds(1, 1)).wait_send()

    @pl.loop(0, jnp.maximum(d - 1, 0))
    def _(target):
        z_copy(target, 0).wait_send()
        z_copy(target, 1).wait_send()

    @pl.when(d > 0)
    def _():
        for p in range(chips):
            next_copy(p).wait_send()

    if depth >= 3:
        @pl.when(d == depth - 1)
        def _():
            for p in range(1, chips):
                far_copy(p).wait_send()


def per_device(depth, count, amplitude, phase, kernel_phase, entry_field, cotangent):
    _, rows, length = amplitude.shape
    angles = entry_field.shape[2]
    assert angles == 1 and amplitude.shape[0] == 1 and count % 2 == 0
    chips, above = count // 2, max(depth - 1, 1)
    wide, tall, shuffle = map(jnp.asarray, tables(length))
    field = (2, length, length)
    blocks = (2, chips, 2, rows, length)
    half_sum = (chips, 2, rows, length)
    dma = pltpu.SemaphoreType.DMA
    return pl.pallas_call(
        functools.partial(kernel, depth, count),
        out_shape=jax.ShapeDtypeStruct((2, 1, rows, length), F32),
        in_specs=[pl.BlockSpec(memory_space=pltpu.HBM)] * 8,
        out_specs=pl.BlockSpec(memory_space=pltpu.VMEM),
        scratch_shapes=[
            pltpu.VMEM((rows, length), F32),
            pltpu.VMEM((rows, length), F32),
            pltpu.VMEM((length, length), F32),
            pltpu.VMEM(blocks, F32),
            pltpu.VMEM(wide.shape, BF16),
            pltpu.VMEM(tall.shape, BF16),
            pltpu.VMEM(shuffle.shape, BF16),
            pltpu.VMEM(field, F32),
            pltpu.VMEM(field, F32),
            pltpu.VMEM((2, length, length // 2), F32),
            pltpu.VMEM((2, rows, length), F32),
            pltpu.VMEM((above, chips, 2, 2, rows, length), F32),
            pltpu.VMEM(blocks, F32),
            pltpu.VMEM(half_sum, F32),
            pltpu.VMEM(half_sum, F32),
            pltpu.VMEM(half_sum, F32),
            pltpu.VMEM(half_sum, F32),
            dma((8,)),
            dma((above, 2)), dma((above, 2)), dma((chips,)), dma((chips,)),
            dma((above, chips, 2)), dma((above, chips)),
            dma((above, chips)), dma((above, chips)),
            dma((chips,)), dma((chips,)), dma((chips,)), dma((chips,)),
        ],
        compiler_params=pltpu.CompilerParams(
            collective_id=0, has_side_effects=True, vmem_limit_bytes=60 * 1024 * 1024),
    )(amplitude[0], phase[0], kernel_phase,
      entry_field.reshape(blocks), cotangent[:, 0], wide, tall, shuffle)


def solution(mesh):
    return jax.shard_map(
        functools.partial(per_device, mesh.shape["depth"], mesh.shape["illum"]),
        mesh=mesh,
        in_specs=(
            P("depth", "illum", None),
            P("depth", "illum", None),
            P(),
            P(None, "depth", "illum", None, None),
            P(None, "illum", None, None),
        ),
        out_specs=P(None, "depth", "illum", None),
        check_vma=False,
    )
```

```python
import functools
import math

import jax
import jax.numpy as jnp
import ml_dtypes
import numpy as np
from jax import lax
from jax.experimental import pallas as pl
from jax.experimental.pallas import tpu as pltpu
from jax.sharding import PartitionSpec as P

MESH = pl.DeviceIdType.MESH
F32 = jnp.float32
BF16 = jnp.bfloat16


def halves(matrix):
    high = matrix.astype(ml_dtypes.bfloat16)
    low = (matrix - high.astype(np.float64)).astype(ml_dtypes.bfloat16)
    return [high, low]


def tables(length):
    half = length // 2
    lefts = []
    for odd in (0, 1):
        k = 2 * np.arange(half)[:, None] + odd
        angle = (k * np.arange(half)[None, :] % length) * (2.0 * np.pi / length)
        c, s = np.cos(angle), np.sin(angle)
        lefts.append(np.block([[c, s], [-s, c]]))
    lefts += [lefts[0].T, lefts[1].T]
    perm = np.concatenate([np.arange(0, length, 2), np.arange(1, length, 2)])
    shuffle = np.zeros((length, length))
    shuffle[perm, np.arange(length)] = 1.0
    wide, tall = [], []
    for high, low in map(halves, lefts):
        wide.append(np.concatenate([high, high, low], axis=1))
    for high, low in map(halves, lefts):
        tall.append(np.concatenate([high, high, low], axis=0))
    return np.stack(wide), np.stack(tall), shuffle.astype(ml_dtypes.bfloat16)


def sincos(x):
    y = x * 0.5
    z = y * y
    s = 1.0 / math.factorial(13)
    for order in (11, 9, 7, 5, 3, 1):
        s = s * z + (-1.0) ** (order // 2) / math.factorial(order)
    s = s * y
    c = 1.0 / math.factorial(12)
    for order in (10, 8, 6, 4, 2, 0):
        c = c * z + (-1.0) ** (order // 2) / math.factorial(order)
    return 2.0 * s * c, 1.0 - 2.0 * s * s


def split(v):
    high = v.astype(BF16)
    return high, (v - high.astype(F32)).astype(BF16)


def dot(a, b):
    return jnp.dot(a, b, preferred_element_type=F32)


def right(v, tab, at):
    high, low = split(v)
    return dot(jnp.concatenate([high, low, high], axis=1), tab[at])


def left(v, tab, at):
    high, low = split(v)
    return dot(tab[at], jnp.concatenate([high, low, high], axis=0))


def kernel(
    depth, count, amp_hbm, phase_hbm, kern_hbm, psi_hbm, cot_hbm, wide_hbm, tall_hbm, shuffle_hbm, out_ref,
    amp_ref, phase_ref, kern_ref, psi_ref, wide, tall, shuffle_ref,
    x_ref, h_ref, tmp_ref, own_ref, t_ref, end_ref, give_ref, got_ref, keep_ref, land_ref, loaded,
    z_send, z_recv, n_send, f_send, g_send, g_recv, c_send, c_recv, twin_send, twin_recv, r_send, r_recv,
):
    length = kern_ref.shape[0]
    half = length // 2
    rows = amp_ref.shape[0]
    chips = count // 2
    d = lax.axis_index("depth")
    me = lax.axis_index("illum")
    chip, core = me // 2, me % 2
    needed = depth - 1 - d

    loads = [
        pltpu.make_async_copy(source, target, loaded.at[i])
        for i, (source, target) in enumerate([
            (amp_hbm, amp_ref), (phase_hbm, phase_ref), (kern_hbm, kern_ref),
            (shuffle_hbm, shuffle_ref), (cot_hbm, x_ref), (tall_hbm, tall),
            (wide_hbm, wide), (psi_hbm, psi_ref)])
    ]
    for load in loads:
        load.start()

    def near(p):
        return (chip + p) % chips

    def owner(p):
        if p < chips:
            return 2 * near(p) + core
        return 2 * near(p - chips) + 1 - core

    twin = (d, 2 * chip + 1 - core)
    barrier = pltpu.get_barrier_semaphore()

    def greet(plane, block):
        pl.semaphore_signal(barrier, inc=1, device_id=(plane, block), device_id_type=MESH)

    @pl.loop(d + 1, depth)
    def _(plane):
        greet(plane, me)

    for p in range(1, chips):
        greet(d, owner(p))

        @pl.when(d < depth - 1)
        def _():
            greet(d + 1, owner(p))

        if depth >= 3:
            @pl.when(d == 0)
            def _():
                greet(depth - 1, owner(p))

    greet(*twin)

    loads[0].wait()
    loads[1].wait()
    sin_t, cos_t = sincos(phase_ref[...])
    own_ref[0] = amp_ref[...] * cos_t
    own_ref[1] = amp_ref[...] * sin_t

    lead = 1 - jnp.minimum(needed, 1)
    peers = jnp.minimum(d, 1) + (lead if depth >= 3 else 0)
    pl.semaphore_wait(barrier, d + (chips - 1) * peers + chips)

    def z_copy(target, c):
        return pltpu.make_async_remote_copy(
            src_ref=own_ref.at[c], dst_ref=t_ref.at[needed, chip, core, c],
            send_sem=z_send.at[target, c], recv_sem=z_recv.at[needed, c],
            device_id=(target, me), device_id_type=MESH,
        )

    def next_copy(p):
        return pltpu.make_async_remote_copy(
            src_ref=own_ref, dst_ref=t_ref.at[needed, chip, core],
            send_sem=n_send.at[p], recv_sem=g_recv.at[needed, (chips - p) % chips],
            device_id=(d - 1, owner(p)), device_id_type=MESH,
        )

    def far_copy(p):
        return pltpu.make_async_remote_copy(
            src_ref=own_ref.at[1], dst_ref=t_ref.at[0, chip, core, 1],
            send_sem=f_send.at[p], recv_sem=g_recv.at[0, chips - p],
            device_id=(0, owner(p)), device_id_type=MESH,
        )

    def z_start(target):
        @pl.when(target < d - 1)
        def _():
            z_copy(target, 0).start()
            if depth >= 3:
                @pl.when(jnp.logical_and(d == depth - 1, target == 0))
                def _():
                    for p in range(1, chips):
                        far_copy(p).start()
            z_copy(target, 1).start()

        @pl.when(target == d - 1)
        def _():
            for p in range(chips):
                next_copy(p).start()

    def post(g):
        target = g + lead

        @pl.when(jnp.logical_and(target >= 0, target < d))
        def _():
            z_start(target)

    post(-1)

    def g_copy(s, p, part):
        half_at = part.start
        block = t_ref.at[s, chip, core, part]
        return pltpu.make_async_remote_copy(
            src_ref=block, dst_ref=block,
            send_sem=g_send.at[s, p, half_at], recv_sem=g_recv.at[s, chips - p],
            device_id=(d, owner(p)), device_id_type=MESH,
        )

    def c_copy(s, p):
        block = t_ref.at[s, near(p), core]
        return pltpu.make_async_remote_copy(
            src_ref=block, dst_ref=block,
            send_sem=c_send.at[s, p], recv_sem=c_recv.at[s, p],
            device_id=twin, device_id_type=MESH,
        )

    def spread(s):
        @pl.when(s < needed - 1)
        def _():
            for c in (0, 1):
                pltpu.make_async_copy(
                    own_ref.at[c], t_ref.at[s, chip, core, c], z_recv.at[s, c]).wait()

                @pl.when(jnp.logical_or(c == 0, jnp.logical_or(s > 0, d > 0)))
                def _():
                    for p in range(1, chips):
                        g_copy(s, p, pl.ds(c, 1)).start()
            c_copy(s, 0).start()

    def pass_on(s, p):
        @pl.when(s < needed if p else s == needed - 1)
        def _():
            pltpu.make_async_copy(own_ref, t_ref.at[s, near(p), core], g_recv.at[s, p]).wait()
            c_copy(s, p).start()

    def pass_all(s):
        spread(s + 1)
        for p in [*range(1, chips), 0]:
            pass_on(s, p)

    def arrived(s):
        for p in range(chips):
            c_copy(s, p).wait_recv()

    loads[2].wait()
    loads[3].wait()
    phase = kern_ref[...]
    first, rest = split(phase)
    rest = phase - first.astype(F32)
    second, third = split(rest)
    shuffle = shuffle_ref[...]
    moved = (dot(third, shuffle) + dot(second, shuffle)) + dot(first, shuffle)
    tmp_ref[0], tmp_ref[1] = moved[:, :half], moved[:, half:]
    scale = 1.0 / (length * length)
    for odd in (0, 1):
        for c in (0, 1):
            sin_h, cos_h = sincos(tmp_ref[c, pl.ds(odd, half, stride=2), :])
            at = (pl.ds(odd * half, half), pl.ds(c * half, half))
            h_ref[(0, *at)] = cos_h * scale
            h_ref[(1, *at)] = sin_h * scale

    for load in loads[4:7]:
        load.wait()

    def propagate(re, im, slot):
        parts = []
        for sign, at in ((1, 2), (-1, 3)):
            mixed = jnp.concatenate(
                [v[:, :half] + sign * v[:, half:] for v in (re, im)], axis=1)
            parts.append(right(mixed, tall, at))
        slot(0)
        even, odd = parts
        back = []
        mixes = []
        for sign, at in ((1, 0), (-1, 1)):
            stack = jnp.concatenate([
                jnp.concatenate([
                    v[:half, c * half:(c + 1) * half] + sign * v[half:, c * half:(c + 1) * half]
                    for v in (even, odd)], axis=1)
                for c in (0, 1)], axis=0)
            freq = left(stack, wide, at)
            f_re, f_im = freq[:half], freq[half:]
            h_re = h_ref[0, at * half:(at + 1) * half]
            h_im = h_ref[1, at * half:(at + 1) * half]
            mixes.append(jnp.concatenate(
                [f_re * h_re + f_im * h_im, f_im * h_re - f_re * h_im], axis=0))
        slot(1)
        for at in (0, 1):
            back.append(left(mixes[at], wide, 2 + at))
        slot(2)
        e, o = back
        total, gap = e + o, e - o
        for c in (0, 1):
            cols = slice(c * half, (c + 1) * half)
            mixed = jnp.concatenate([
                jnp.concatenate([total[:half, cols], gap[:half, cols]], axis=0),
                jnp.concatenate([total[half:, cols], gap[half:, cols]], axis=0)], axis=1)
            end_ref[c] = mixed.reshape(chips, 2, rows, length)

    def finish(ends):
        e, o = [right(v, tall, at) for at, v in enumerate(ends)]
        total, gap = e + o, e - o
        return (
            jnp.concatenate([total[:, :half], gap[:, :half]], axis=1),
            jnp.concatenate([total[:, half:], gap[:, half:]], axis=1),
        )

    def first_slot(k):
        post(k)
        if k == 0:
            spread(0)
        elif k == 1:
            pass_all(0)

    propagate(x_ref[0], x_ref[1], first_slot)

    @pl.loop(jnp.minimum(3 + lead, d), d)
    def _(target):
        z_start(target)

    def body(q, carry):
        def slot(k):
            if k == 1:
                pass_all(q + 1)

        u_re, u_im = finish([end_ref[c].reshape(length, length) for c in (0, 1)])
        arrived(q)
        t_re, t_im = [t_ref[q, :, :, c].reshape(length, length) for c in (0, 1)]
        propagate(u_re * t_re + u_im * t_im, u_im * t_re - u_re * t_im, slot)
        return carry

    lax.fori_loop(0, needed, body, 0)

    def products(to_ref, kind):
        flat = (chips * rows, length)
        u_re, u_im = finish([end_ref[c, :, kind].reshape(flat) for c in (0, 1)])
        p_re, p_im = [psi_ref[c, :, kind].reshape(flat) for c in (0, 1)]
        shape = (chips, rows, length)
        to_ref[:, 0] = (u_re * p_re + u_im * p_im).reshape(shape)
        to_ref[:, 1] = (u_im * p_re - u_re * p_im).reshape(shape)

    def twin_copy(p):
        at = near(p)
        return pltpu.make_async_remote_copy(
            src_ref=give_ref.at[at], dst_ref=got_ref.at[at],
            send_sem=twin_send.at[p], recv_sem=twin_recv.at[p],
            device_id=twin, device_id_type=MESH,
        )

    def sum_copy(p):
        return pltpu.make_async_remote_copy(
            src_ref=keep_ref.at[near(p)], dst_ref=land_ref.at[chips - p],
            send_sem=r_send.at[p], recv_sem=r_recv.at[chips - p],
            device_id=(d, owner(p)), device_id_type=MESH,
        )

    loads[7].wait()
    products(give_ref, 1 - core)
    order = [*range(1, chips), 0]
    for p in order:
        twin_copy(p).start()
    products(keep_ref, core)
    for p in order:
        twin_copy(p).wait_recv()
        if p:
            keep_ref[near(p)] += got_ref[near(p)]
            sum_copy(p).start()
    total = keep_ref[chip] + got_ref[chip]
    for p in range(1, chips):
        pltpu.make_async_copy(own_ref, land_ref.at[p], r_recv.at[p]).wait()
        total = total + land_ref[p]
    out_ref[:, 0] = total * (1.0 / math.sqrt(count))

    for p in range(chips):
        twin_copy(p).wait_send()
        if p:
            sum_copy(p).wait_send()

    @pl.loop(0, needed)
    def _(s):
        for p in range(chips):
            c_copy(s, p).wait_send()

    @pl.loop(0, jnp.maximum(needed - 1, 0))
    def _(s):
        for p in range(1, chips):
            g_copy(s, p, pl.ds(0, 1)).wait_send()

            @pl.when(jnp.logical_or(s > 0, d > 0))
            def _():
                g_copy(s, p, pl.ds(1, 1)).wait_send()

    @pl.loop(0, jnp.maximum(d - 1, 0))
    def _(target):
        z_copy(target, 0).wait_send()
        z_copy(target, 1).wait_send()

    @pl.when(d > 0)
    def _():
        for p in range(chips):
            next_copy(p).wait_send()

    if depth >= 3:
        @pl.when(d == depth - 1)
        def _():
            for p in range(1, chips):
                far_copy(p).wait_send()


def per_device(depth, count, amplitude, phase, kernel_phase, entry_field, cotangent):
    _, rows, length = amplitude.shape
    angles = entry_field.shape[2]
    assert angles == 1 and amplitude.shape[0] == 1 and count % 2 == 0
    chips, above = count // 2, max(depth - 1, 1)
    wide, tall, shuffle = map(jnp.asarray, tables(length))
    field = (2, length, length)
    blocks = (2, chips, 2, rows, length)
    half_sum = (chips, 2, rows, length)
    dma = pltpu.SemaphoreType.DMA
    return pl.pallas_call(
        functools.partial(kernel, depth, count),
        out_shape=jax.ShapeDtypeStruct((2, 1, rows, length), F32),
        in_specs=[pl.BlockSpec(memory_space=pltpu.HBM)] * 8,
        out_specs=pl.BlockSpec(memory_space=pltpu.VMEM),
        scratch_shapes=[
            pltpu.VMEM((rows, length), F32),
            pltpu.VMEM((rows, length), F32),
            pltpu.VMEM((length, length), F32),
            pltpu.VMEM(blocks, F32),
            pltpu.VMEM(wide.shape, BF16),
            pltpu.VMEM(tall.shape, BF16),
            pltpu.VMEM(shuffle.shape, BF16),
            pltpu.VMEM(field, F32),
            pltpu.VMEM(field, F32),
            pltpu.VMEM((2, length, length // 2), F32),
            pltpu.VMEM((2, rows, length), F32),
            pltpu.VMEM((above, chips, 2, 2, rows, length), F32),
            pltpu.VMEM(blocks, F32),
            pltpu.VMEM(half_sum, F32),
            pltpu.VMEM(half_sum, F32),
            pltpu.VMEM(half_sum, F32),
            pltpu.VMEM(half_sum, F32),
            dma((8,)),
            dma((above, 2)), dma((above, 2)), dma((chips,)), dma((chips,)),
            dma((above, chips, 2)), dma((above, chips)),
            dma((above, chips)), dma((above, chips)),
            dma((chips,)), dma((chips,)), dma((chips,)), dma((chips,)),
        ],
        compiler_params=pltpu.CompilerParams(
            collective_id=0, has_side_effects=True, vmem_limit_bytes=60 * 1024 * 1024),
    )(amplitude[0], phase[0], kernel_phase,
      entry_field.reshape(blocks), cotangent[:, 0], wide, tall, shuffle)


def solution(mesh):
    return jax.shard_map(
        functools.partial(per_device, mesh.shape["depth"], mesh.shape["illum"]),
        mesh=mesh,
        in_specs=(
            P("depth", "illum", None),
            P("depth", "illum", None),
            P(),
            P(None, "depth", "illum", None, None),
            P(None, "illum", None, None),
        ),
        out_specs=P(None, "depth", "illum", None),
        check_vma=False,
    )
```
